256 devices in a mesh: seq: 64 (over y_lo, z, x), head: 4 (over y_hi, core).
Axes of the slice: x: 4, y: 4 (y_hi: 2, y_lo: 2; y = y_hi * 2 + y_lo), z: 8, core: 2. Of those that a mesh axis runs over, the one named last changes fastest.
Arguments:
- queries: bfloat16 [65536, 4096], P('seq', 'head'), may hold values from -120 to 120
- keys: bfloat16 [65536, 512], P('seq', 'head'), may hold values from -6 to 6
- values: bfloat16 [65536, 512], P('seq', 'head'), may hold values from -6 to 6
- mid_pool: bfloat16 [4, 8], P('head'), may hold values from -3 to 3
- coarse_pool: bfloat16 [4, 256], P('head'), may hold values from -0.375 to 0.375
Outputs:
- attended: bfloat16 [65536, 4096], P(('seq', 'head'))
The draws below stay inside these ranges and needn't reach their ends.
All inputs are finite; a program needn't handle non-finite values.
Results may differ from the reference program's by a relative error of at most 0.0092.
Values may be sent and summed in bfloat16 or wider, within the bound.
A program may use at most 128 MiB of HBM per device.

```python
import math
import jax
import jax.numpy as jnp
from jax import lax

HEADS = 32
KV_GROUP = 8
HEAD_DIM = 128
BLK = 256
GROUP = 8
MIDS = 256
KV_HEADS = 4
MIDB = 8
SEQ = 65536


def joint_draw(key):
    base = jax.random.fold_in(key, 7)
    subkeys = jax.random.split(base, 2)
    query = jax.random.truncated_normal(subkeys[0], -6.0, 6.0, (SEQ, HEADS, HEAD_DIM), jnp.float32)
    keyset = jax.random.truncated_normal(subkeys[1], -6.0, 6.0, (SEQ, KV_HEADS, HEAD_DIM), jnp.float32)
    return (query.reshape(SEQ, HEADS * HEAD_DIM), keyset.reshape(SEQ, KV_HEADS * HEAD_DIM))


def draw_queries(key, part):
    return joint_draw(key)[0].astype(jnp.bfloat16)


def draw_keys(key, part):
    return joint_draw(key)[1].astype(jnp.bfloat16)


def levels(rng, shape, cuts, smallest, largest):
    def one(dim, parts):
        heights = jax.random.uniform(jax.random.fold_in(jax.random.fold_in(rng, 6), dim), (parts,), jnp.float32, smallest / len(cuts), largest / len(cuts))
        return jnp.repeat(jnp.exp(heights), shape[dim] // parts).reshape((-1,) + (1,) * (len(shape) - dim - 1))

    level = one(*cuts[0])
    for cut in cuts[1:]:
        level = level * one(*cut)
    return level


def noise(stream_key, extent, deviation, limit, cuts=(), kind=jnp.bfloat16):
    result = jax.random.normal(stream_key, extent, jnp.float32) * deviation
    if len(cuts) > 0:
        result = levels(stream_key, extent, cuts, -0.22, 0.18) * result
    return jnp.clip(result, min=-limit, max=limit).astype(kind)


def setup_inputs(seed: int = 0) -> dict:
    key_of = jax.random.split(jax.random.key(seed), 6)
    return {
        "queries": draw_queries(jax.random.fold_in(key_of[5], 71), 0),
        "keys": draw_keys(jax.random.fold_in(key_of[5], 71), 0),
        "values": noise(key_of[2], (SEQ, KV_HEADS * HEAD_DIM), 1.0, 6.0, ((0, 64), (1, 4))),
        "mid_pool": noise(key_of[3], (KV_HEADS, GROUP), 0.5, 3.0, ((0, 4),)),
        "coarse_pool": noise(key_of[4], (KV_HEADS, BLK), (BLK ** -0.5), 0.375, ((0, 4),)),
    }


def reference(queries, keys, values, mid_pool, coarse_pool):
    seq_len = queries.shape[0]
    blocks = seq_len // BLK
    per_group = BLK // GROUP
    logit_scale = 1.0 / math.sqrt(HEAD_DIM)

    def one_head(head_index):
        kv_index = head_index // KV_GROUP
        column = head_index * HEAD_DIM
        kv_column = kv_index * HEAD_DIM
        head_query = lax.dynamic_slice_in_dim(queries, column, HEAD_DIM, 1)
        head_key = lax.dynamic_slice_in_dim(keys, kv_column, HEAD_DIM, 1)
        head_value = lax.dynamic_slice_in_dim(values, kv_column, HEAD_DIM, 1)
        mid_weights = lax.dynamic_slice_in_dim(mid_pool, kv_index, 1, 0)[0].astype(jnp.float32)
        coarse_weights = lax.dynamic_slice_in_dim(coarse_pool, kv_index, 1, 0)[0].astype(jnp.float32)

        def pooled(source, weights, group_size):
            grouped = source.astype(jnp.float32).reshape(seq_len // group_size, group_size, HEAD_DIM)
            return jnp.einsum('gtd,t->gd', grouped, weights).astype(jnp.bfloat16)
        mid_keys = pooled(head_key, mid_weights, GROUP)
        mid_values = pooled(head_value, mid_weights, GROUP)
        summary_key_rows = pooled(head_key, coarse_weights, BLK)
        coarse_values = pooled(head_value, coarse_weights, BLK)
        zero_rows = jnp.zeros((BLK, HEAD_DIM), jnp.bfloat16)
        key_blocks = jnp.concatenate([zero_rows, head_key]).reshape(blocks + 1, BLK, HEAD_DIM)
        value_blocks = jnp.concatenate([zero_rows, head_value]).reshape(blocks + 1, BLK, HEAD_DIM)
        local_keys = jnp.concatenate([key_blocks[:-1], key_blocks[1:]], axis=1)
        near_values = jnp.concatenate([value_blocks[:-1], value_blocks[1:]], axis=1)
        zero_groups = jnp.zeros(((MIDB + 1) * per_group, HEAD_DIM), jnp.bfloat16)
        mid_padded_k = jnp.concatenate([zero_groups, mid_keys]).reshape(blocks + MIDB + 1, per_group, HEAD_DIM)
        mid_padded_v = jnp.concatenate([zero_groups, mid_values]).reshape(blocks + MIDB + 1, per_group, HEAD_DIM)
        distant_keys = jnp.concatenate([mid_padded_k[offset:offset + blocks] for offset in range(MIDB)], axis=1)
        far_v = jnp.concatenate([mid_padded_v[offset:offset + blocks] for offset in range(MIDB)], axis=1)
        blocked_queries = head_query.astype(jnp.float32).reshape(blocks, BLK, HEAD_DIM)
        local_scores = jnp.einsum('hwu,hau->hwa', blocked_queries, local_keys.astype(jnp.float32)) * logit_scale
        middle_level_scores = jnp.einsum('hwu,hau->hwa', blocked_queries, distant_keys.astype(jnp.float32)) * logit_scale
        summary_score_rows = jnp.einsum('ipj,xj->ipx', blocked_queries, summary_key_rows.astype(jnp.float32)) * logit_scale
        block_ids = jnp.arange(blocks, dtype=jnp.int32)[:, None, None]
        query_pos = block_ids * BLK + jnp.arange(BLK, dtype=jnp.int32)[None, :, None]
        key_pos = block_ids * BLK - BLK + jnp.arange(2 * BLK, dtype=jnp.int32)[None, None, :]
        near_ok = (key_pos >= 0) & (key_pos <= query_pos)
        mid_ok = (block_ids - 1 - MIDB) * per_group + jnp.arange(MIDS, dtype=jnp.int32)[None, None, :] >= 0
        coarse_ok = jnp.arange(blocks, dtype=jnp.int32)[None, None, :] <= block_ids - MIDB - 2
        scores = jnp.concatenate([jnp.where(near_ok, local_scores, -jnp.inf), jnp.where(mid_ok, middle_level_scores, -jnp.inf), jnp.where(coarse_ok, summary_score_rows, -jnp.inf)], axis=-1)
        row_max = lax.optimization_barrier(jnp.max(scores, axis=-1, keepdims=True))
        exponent = jnp.exp(scores - row_max)
        row_total = lax.optimization_barrier(jnp.sum(exponent, axis=-1, keepdims=True))
        softmax_weights = (exponent / row_total).astype(jnp.bfloat16)
        coarse_all = jnp.broadcast_to(coarse_values[None], (blocks, blocks, HEAD_DIM))
        collected_rows = jnp.concatenate([near_values, far_v, coarse_all], axis=1)
        output_rows = jnp.einsum('sja,sah->sjh', softmax_weights.astype(jnp.float32), collected_rows.astype(jnp.float32))
        return output_rows.astype(jnp.bfloat16).reshape(seq_len, HEAD_DIM)
    every_head = lax.map(one_head, jnp.arange(HEADS, dtype=jnp.int32))
    return jnp.transpose(every_head, (1, 0, 2)).reshape(seq_len, HEADS * HEAD_DIM)
```

```python
import math

import jax
import jax.numpy as jnp
from jax import lax
from jax.experimental import pallas as pl
from jax.experimental.pallas import tpu as pltpu
from jax.sharding import PartitionSpec as P

HEAD_DIM = 128
BLK = 256
GROUP = 8
PER = BLK // GROUP
MIDB = 8
MIDS = 256
HERE = 4
CLAN = 8
UNROLL = 4
MESH = pl.DeviceIdType.MESH
BF = jnp.bfloat16
F32 = jnp.float32
SCALE = math.log2(math.e) / math.sqrt(HEAD_DIM)


def nt(a, b):
    return lax.dot_general(a, b, (((1,), (1,)), ((), ())), preferred_element_type=F32)


def mm(a, b):
    return jnp.dot(a, b, preferred_element_type=F32)


def iota(shape, dim):
    return lax.broadcasted_iota(jnp.int32, shape, dim)


def pool_matrix(mid_ref, coarse_ref):
    row, col = iota((48, BLK), 0), iota((48, BLK), 1)
    mids = mid_ref[...].astype(F32)
    spread = jnp.zeros((1, BLK), F32)
    lane = iota((1, BLK), 1) % GROUP
    for t in range(GROUP):
        spread = jnp.where(lane == t, mids[0:1, t : t + 1], spread)
    w = jnp.where((row < PER) & (col // GROUP == row), spread, 0.0)
    return jnp.where(row == PER, coarse_ref[...].astype(F32), w).astype(BF)


def kernel(
    queries,
    keys,
    values,
    mid_pool,
    coarse_pool,
    out,
    qb,
    ob,
    near,
    mymid,
    mid,
    coarse,
    unit,
    in_sem,
    q_sem,
    halo_s,
    halo_r,
    one_s,
    one_r,
    two_s,
    two_r,
    out_s,
    out_r,
):
    s, h = lax.axis_index("seq"), lax.axis_index("head")
    devices = lax.axis_size("seq")
    clans = devices // CLAN
    a, b = s // CLAN, s % CLAN
    yh, core = h // 2, h % 2

    def target(i):
        fy, fc = 1 - i // 2, ((i + 1) // 2) % 2
        return ((yh + fy) % 2) * 2 + (core + fc) % 2

    loads = [
        pltpu.make_async_copy(keys, near.at[pl.ds(BLK, HERE * BLK), pl.ds(0, HEAD_DIM)], in_sem.at[0]),
        pltpu.make_async_copy(
            values, near.at[pl.ds(BLK, HERE * BLK), pl.ds(HEAD_DIM, HEAD_DIM)], in_sem.at[1]
        ),
    ]
    for c in loads:
        c.start()

    def q_load(i):
        return pltpu.make_async_copy(
            queries.at[pl.ds(pl.multiple_of(target(i) * BLK, BLK), BLK)], qb.at[i], q_sem.at[i]
        )

    for i in range(HERE):
        q_load(i).start()

    near[0:BLK, 0 : 2 * HEAD_DIM] = jnp.zeros((BLK, 2 * HEAD_DIM), BF)
    mid[0:288, 0 : 2 * HEAD_DIM] = jnp.zeros((288, 2 * HEAD_DIM), BF)
    coarse[:, 0 : 2 * HEAD_DIM] = jnp.zeros((coarse.shape[0], 2 * HEAD_DIM), BF)

    barrier = pltpu.get_barrier_semaphore()

    def tell(seq, head):
        pl.semaphore_signal(barrier, inc=1, device_id=(seq, head), device_id_type=MESH)

    for i in range(3):
        tell(s, target(i))
    for i in range(1, CLAN):
        tell(a * CLAN + (b + i) % CLAN, h)
    for back in (1, 2, 3):

        @pl.when(s >= back)
        def _():
            tell(s - back, h)

    def tell_lower(k, carry):
        tell(k * CLAN + b, h)
        return carry

    lax.fori_loop(0, a, tell_lower, 0)

    near[:, 2 * HEAD_DIM :] = jnp.ones((near.shape[0], HEAD_DIM), BF)
    mid[:, 2 * HEAD_DIM :] = jnp.ones((mid.shape[0], HEAD_DIM), BF)
    coarse[:, 2 * HEAD_DIM :] = jnp.ones((coarse.shape[0], HEAD_DIM), BF)
    pooling = pool_matrix(mid_pool, coarse_pool)
    for c in loads:
        c.wait()
    tops = []
    for j in range(HERE):
        pooled = mm(pooling, near[BLK + j * BLK : 2 * BLK + j * BLK, 0 : 2 * HEAD_DIM])
        mymid[j * PER : (j + 1) * PER, :] = pooled[0:PER].astype(BF)
        if j < 2:
            mid[288 + j * PER : 288 + (j + 1) * PER, 0 : 2 * HEAD_DIM] = pooled[0:PER].astype(BF)
        tops.append(pooled[PER : PER + 1])
    rows = [t[:, :HEAD_DIM] for t in tops] + [t[:, HEAD_DIM:] for t in tops]
    mine = jnp.zeros((16, HEAD_DIM), F32)
    for n, r in enumerate(rows):
        mine = jnp.where(iota((16, HEAD_DIM), 0) == n, r, mine)
    unit[b] = mine.astype(BF)

    pl.semaphore_wait(barrier, 3 + (CLAN - 1) + (clans - 1 - a) + jnp.minimum(3, devices - 1 - s))

    def one(i):
        return pltpu.make_async_remote_copy(
            src_ref=unit.at[b],
            dst_ref=unit.at[b],
            send_sem=one_s.at[i],
            recv_sem=one_r.at[i],
            device_id=(a * CLAN + (b + i) % CLAN, h),
            device_id_type=MESH,
        )

    def halo(n):
        src, dst, step = (
            (near.at[pl.ds(HERE * BLK, BLK), pl.ds(0, 256)], near.at[pl.ds(0, BLK), pl.ds(0, 256)], 1),
            (mymid, mid.at[pl.ds(160, 128), pl.ds(0, 256)], 1),
            (mymid, mid.at[pl.ds(32, 128), pl.ds(0, 256)], 2),
            (mymid.at[pl.ds(96, 32)], mid.at[pl.ds(0, 32), pl.ds(0, 256)], 3),
        )[n]
        copy = pltpu.make_async_remote_copy(
            src_ref=src,
            dst_ref=dst,
            send_sem=halo_s.at[n],
            recv_sem=halo_r.at[n],
            device_id=(s + step, h),
            device_id_type=MESH,
        )
        return copy, step

    def two(k):
        block = coarse.at[pl.ds(pl.multiple_of(a * 32, 32), 32), pl.ds(0, 256)]
        return pltpu.make_async_remote_copy(
            src_ref=block,
            dst_ref=block,
            send_sem=two_s.at[k],
            recv_sem=two_r.at[a],
            device_id=(k * CLAN + b, h),
            device_id_type=MESH,
        )

    def two_from(k):
        block = coarse.at[pl.ds(pl.multiple_of(k * 32, 32), 32), pl.ds(0, 256)]
        return pltpu.make_async_remote_copy(
            src_ref=block,
            dst_ref=block,
            send_sem=two_s.at[a],
            recv_sem=two_r.at[k],
            device_id=(k * CLAN + b, h),
            device_id_type=MESH,
        )

    for i in range(1, CLAN):
        one(i).start()
    for n in range(4):
        copy, step = halo(n)
        pl.when(s + step < devices)(copy.start)
    for i in range(1, CLAN):
        one(i).wait()
    units = unit[...].reshape(CLAN * 16, HEAD_DIM)
    r, c = iota((32, CLAN * 16), 0), iota((32, CLAN * 16), 1)
    at = (r // HERE) * 16 + r % HERE
    pick_k = jnp.where(c == at, 1.0, 0.0).astype(BF)
    pick_v = jnp.where(c == at + HERE, 1.0, 0.0).astype(BF)
    clan_rows = pl.ds(pl.multiple_of(a * 32, 32), 32)
    coarse[clan_rows, 0:HEAD_DIM] = mm(pick_k, units).astype(BF)
    coarse[clan_rows, HEAD_DIM : 2 * HEAD_DIM] = mm(pick_v, units).astype(BF)

    def start_two(k, carry):
        two(k).start()
        return carry

    lax.fori_loop(a + 1, clans, start_two, 0)
    for n in range(4):
        copy, step = halo(n)
        pl.when(s >= step)(copy.wait_recv)

    def got_two(k, carry):
        two_from(k).wait_recv()
        return carry

    lax.fori_loop(0, a, got_two, 0)
    for i in range(HERE):
        q_load(i).wait()

    wide = UNROLL * HEAD_DIM
    halves = qb.shape[2] // wide

    def sent(i, g):
        return pltpu.make_async_remote_copy(
            src_ref=ob.at[i, :, pl.ds(pl.multiple_of(g * wide, wide), wide)],
            dst_ref=out.at[:, pl.ds(pl.multiple_of(h * qb.shape[2] + g * wide, wide), wide)],
            send_sem=out_s.at[i, g],
            recv_sem=out_r.at[i, g],
            device_id=(s, target(i)),
            device_id_type=MESH,
        )

    def kept(g):
        return pltpu.make_async_copy(
            ob.at[3, :, pl.ds(pl.multiple_of(g * wide, wide), wide)],
            out.at[:, pl.ds(pl.multiple_of(h * qb.shape[2] + g * wide, wide), wide)],
            out_s.at[3, g],
        )

    causal = iota((BLK, BLK), 1) <= iota((BLK, BLK), 0)

    def step(t, carry):
        i, g = t // halves, t % halves
        j = target(i)
        block = s * HERE + j
        r0 = pl.multiple_of(j * BLK, BLK)
        m0 = pl.multiple_of(j * PER, PER)
        before = jnp.where(block >= 1, 0.0, -jnp.inf)
        mid_bias = jnp.where((block - 1 - MIDB) * PER + iota((1, MIDS), 1) >= 0, 0.0, -jnp.inf)
        coarse_bias = jnp.where(iota((1, coarse.shape[0]), 1) <= block - MIDB - 2, 0.0, -jnp.inf)
        for u in range(UNROLL):
            col = pl.multiple_of((g * UNROLL + u) * HEAD_DIM, HEAD_DIM)
            q = qb[i, :, pl.ds(col, HEAD_DIM)]
            s1 = nt(q, near[pl.ds(r0, BLK), 0:HEAD_DIM]) + before
            s2 = nt(q, near[pl.ds(r0 + BLK, BLK), 0:HEAD_DIM])
            s2 = jnp.where(causal, s2, -jnp.inf)
            s3 = nt(q, mid[pl.ds(m0, MIDS), 0:HEAD_DIM]) + mid_bias
            s4 = nt(q, coarse[:, 0:HEAD_DIM]) + coarse_bias
            top = jnp.maximum(jnp.maximum(s1, s2), jnp.maximum(s3, s4))
            top = jnp.max(top, axis=1, keepdims=True) * SCALE
            p1, p2, p3, p4 = [jnp.exp2(x * SCALE - top).astype(BF) for x in (s1, s2, s3, s4)]
            o = mm(p1, near[pl.ds(r0, BLK), HEAD_DIM:]) + mm(p2, near[pl.ds(r0 + BLK, BLK), HEAD_DIM:])
            o = o + mm(p3, mid[pl.ds(m0, MIDS), HEAD_DIM:]) + mm(p4, coarse[:, HEAD_DIM:])
            ob[i, :, pl.ds(col, HEAD_DIM)] = (o[:, :HEAD_DIM] / o[:, HEAD_DIM:]).astype(BF)

        @pl.when(i < 3)
        def _():
            sent(i, g).start()

        @pl.when(i == 3)
        def _():
            kept(g).start()

        return carry

    lax.fori_loop(0, HERE * halves, step, 0)

    for n in range(4):
        copy, step_up = halo(n)
        pl.when(s + step_up < devices)(copy.wait_send)

    def sent_two(k, carry):
        two(k).wait_send()
        return carry

    lax.fori_loop(a + 1, clans, sent_two, 0)
    for g in range(halves):
        for i in range(3):
            sent(i, g).wait()
        kept(g).wait()


def body(queries, keys, values, mid_pool, coarse_pool):
    rows, columns = queries.shape
    devices = lax.axis_size("seq")
    halves = columns // (UNROLL * HEAD_DIM)
    dma = pltpu.SemaphoreType.DMA
    any_, vmem = pl.BlockSpec(memory_space=pl.ANY), pl.BlockSpec(memory_space=pltpu.VMEM)
    return pl.pallas_call(
        kernel,
        out_shape=jax.ShapeDtypeStruct((rows // HERE, HERE * columns), BF),
        in_specs=[any_, any_, any_, vmem, vmem],
        out_specs=any_,
        scratch_shapes=[
            pltpu.VMEM((HERE, BLK, columns), BF),
            pltpu.VMEM((HERE, BLK, columns), BF),
            pltpu.VMEM(((HERE + 1) * BLK, 384), BF),
            pltpu.VMEM((HERE * PER, 256), BF),
            pltpu.VMEM((352, 384), BF),
            pltpu.VMEM((devices * HERE, 384), BF),
            pltpu.VMEM((CLAN, 16, HEAD_DIM), BF),
            dma((2,)),
            dma((HERE,)),
            dma((4,)),
            dma((4,)),
            dma((CLAN,)),
            dma((CLAN,)),
            dma((devices // CLAN,)),
            dma((devices // CLAN,)),
            dma((4, halves)),
            dma((3, halves)),
        ],
        compiler_params=pltpu.CompilerParams(
            collective_id=0, has_side_effects=True, vmem_limit_bytes=48 * 2**20
        ),
    )(queries, keys, values, mid_pool, coarse_pool)


def solution(mesh):
    return jax.shard_map(
        body,
        mesh=mesh,
        in_specs=(
            P("seq", "head"),
            P("seq", "head"),
            P("seq", "head"),
            P("head", None),
            P("head", None),
        ),
        out_specs=P(("seq", "head"), None),
        check_vma=False,
    )
```

```python
import math

import jax
import jax.numpy as jnp
from jax import lax
from jax.experimental import pallas as pl
from jax.experimental.pallas import tpu as pltpu
from jax.sharding import PartitionSpec as P

HEAD_DIM = 128
BLK = 256
GROUP = 8
PER = BLK // GROUP
MIDB = 8
MIDS = 256
HERE = 4
X, Z, Y = 4, 8, 2
PLANE = X * Y
ROWS = PLANE * HERE
UNROLL = 4
MESH = pl.DeviceIdType.MESH
BF = jnp.bfloat16
F32 = jnp.float32
SCALE = math.log2(math.e) / math.sqrt(HEAD_DIM)


def nt(a, b):
    return lax.dot_general(a, b, (((1,), (1,)), ((), ())), preferred_element_type=F32)


def mm(a, b):
    return jnp.dot(a, b, preferred_element_type=F32)


def iota(shape, dim):
    return lax.broadcasted_iota(jnp.int32, shape, dim)


def pool_matrix(mid_ref, coarse_ref):
    row, col = iota((48, BLK), 0), iota((48, BLK), 1)
    mids = mid_ref[...].astype(F32)
    spread = jnp.zeros((1, BLK), F32)
    lane = iota((1, BLK), 1) % GROUP
    for t in range(GROUP):
        spread = jnp.where(lane == t, mids[0:1, t : t + 1], spread)
    w = jnp.where((row < PER) & (col // GROUP == row), spread, 0.0)
    return jnp.where(row == PER, coarse_ref[...].astype(F32), w).astype(BF)


def kernel(
    queries,
    keys,
    values,
    mid_pool,
    coarse_pool,
    out,
    qb,
    ob,
    near,
    mymid,
    mid,
    coarse,
    unit,
    mid_w,
    coarse_w,
    in_sem,
    q_sem,
    halo_s,
    halo_r,
    one_s,
    one_r,
    two_s,
    two_r,
    ready_near,
    ready_far,
    out_s,
    out_r,
):
    s, h = lax.axis_index("seq"), lax.axis_index("head")
    devices = lax.axis_size("seq")
    y, z, x = s // (Z * X), (s // X) % Z, s % X
    u = y * X + x
    yh, core = h // 2, h % 2
    early = z < Z // 2

    def in_plane(i):
        v = (u + i) % PLANE
        return (v // X) * (Z * X) + z * X + v % X

    def at_z(k):
        return (y * Z + k) * X + x

    def target(i):
        fy, fc = 1 - i // 2, ((i + 1) // 2) % 2
        return ((yh + fy) % 2) * 2 + (core + fc) % 2

    loads = [
        pltpu.make_async_copy(keys, near.at[pl.ds(BLK, HERE * BLK), pl.ds(0, HEAD_DIM)], in_sem.at[0]),
        pltpu.make_async_copy(
            values, near.at[pl.ds(BLK, HERE * BLK), pl.ds(HEAD_DIM, HEAD_DIM)], in_sem.at[1]
        ),
        pltpu.make_async_copy(mid_pool, mid_w, in_sem.at[2]),
        pltpu.make_async_copy(coarse_pool, coarse_w, in_sem.at[3]),
    ]
    for c in loads:
        c.start()

    def q_load(i):
        return pltpu.make_async_copy(
            queries.at[pl.ds(pl.multiple_of(target(i) * BLK, BLK), BLK)], qb.at[i], q_sem.at[i]
        )

    barrier = pltpu.get_barrier_semaphore()

    def tell(seq, head):
        pl.semaphore_signal(barrier, inc=1, device_id=(seq, head), device_id_type=MESH)

    for i in range(3):
        tell(s, target(i))
    for i in range(1, PLANE):
        tell(in_plane(i), h)
    for back in (1, 2, 3):

        @pl.when(s >= back)
        def _():
            tell(s - back, h)

    def tell_upper(k, carry):
        tell(at_z(k), h)
        return carry

    lax.fori_loop(z + 1, Z, tell_upper, 0)

    def blank(ref, start, size):
        ref[pl.ds(start, size), 0 : 2 * HEAD_DIM] = jnp.zeros((size, 2 * HEAD_DIM), BF)

    pl.when(s < 1)(lambda: blank(near, 0, BLK))
    pl.when(s < 1)(lambda: blank(mid, 160, 128))
    pl.when(s < 2)(lambda: blank(mid, 32, 128))
    pl.when(s < 3)(lambda: blank(mid, 0, 32))

    def blank_coarse(k, carry):
        blank(coarse, pl.multiple_of(k * ROWS, ROWS), ROWS)
        return carry

    lax.fori_loop(jnp.where(y == 0, z + 1, Z), Z, blank_coarse, 0)

    near[:, 2 * HEAD_DIM :] = jnp.ones((near.shape[0], HEAD_DIM), BF)
    mid[:, 2 * HEAD_DIM :] = jnp.ones((mid.shape[0], HEAD_DIM), BF)
    coarse[:, 2 * HEAD_DIM :] = jnp.ones((coarse.shape[0], HEAD_DIM), BF)
    for c in loads:
        c.wait()
    for i in range(HERE):
        q_load(i).start()
    pooling = pool_matrix(mid_w, coarse_w)
    tops = []
    for j in range(HERE):
        pooled = mm(pooling, near[BLK + j * BLK : 2 * BLK + j * BLK, 0 : 2 * HEAD_DIM])
        mymid[j * PER : (j + 1) * PER, :] = pooled[0:PER].astype(BF)
        if j < 2:
            mid[288 + j * PER : 288 + (j + 1) * PER, 0 : 2 * HEAD_DIM] = pooled[0:PER].astype(BF)
        tops.append(pooled[PER : PER + 1])
    rows = [t[:, :HEAD_DIM] for t in tops] + [t[:, HEAD_DIM:] for t in tops]
    mine = jnp.zeros((16, HEAD_DIM), F32)
    for n, r in enumerate(rows):
        mine = jnp.where(iota((16, HEAD_DIM), 0) == n, r, mine)
    unit[u] = mine.astype(BF)

    pl.semaphore_wait(barrier, 3 + (PLANE - 1) + z + jnp.minimum(3, devices - 1 - s))

    half = z - z % (Z // 2)

    def tell_ready(sem):
        def tell_one(k, carry):
            pl.semaphore_signal(sem, inc=1, device_id=(at_z(k), h), device_id_type=MESH)
            return carry

        return tell_one

    lax.fori_loop(half, z, tell_ready(ready_near), 0)
    lax.fori_loop(0, half, tell_ready(ready_far), 0)

    def one(i):
        return pltpu.make_async_remote_copy(
            src_ref=unit.at[u],
            dst_ref=unit.at[u],
            send_sem=one_s,
            recv_sem=one_r,
            device_id=(in_plane(i), h),
            device_id_type=MESH,
        )

    def halo(n):
        src, dst, step = (
            (mymid, mid.at[pl.ds(160, 128), pl.ds(0, 256)], 1),
            (mymid, mid.at[pl.ds(32, 128), pl.ds(0, 256)], 2),
            (mymid.at[pl.ds(96, 32)], mid.at[pl.ds(0, 32), pl.ds(0, 256)], 3),
            (near.at[pl.ds(HERE * BLK, BLK), pl.ds(0, 256)], near.at[pl.ds(0, BLK), pl.ds(0, 256)], 1),
        )[n]
        copy = pltpu.make_async_remote_copy(
            src_ref=src,
            dst_ref=dst,
            send_sem=halo_s.at[n],
            recv_sem=halo_r.at[n],
            device_id=(s + step, h),
            device_id_type=MESH,
        )
        return copy, step

    def plane_rows(k):
        return pl.ds(pl.multiple_of(k * ROWS, ROWS), ROWS)

    def two(k, of):
        block = coarse.at[plane_rows(of), pl.ds(0, 256)]
        return pltpu.make_async_remote_copy(
            src_ref=block,
            dst_ref=block,
            send_sem=two_s.at[k],
            recv_sem=two_r.at[of],
            device_id=(at_z(k), h),
            device_id_type=MESH,
        )

    for i in range(1, PLANE):
        one(i).start()
    for n in range(3):
        copy, step = halo(n)
        pl.when(s + step < devices)(copy.start)
    others = unit.at[pl.ds(0, PLANE - 1)]
    all_ones = pltpu.make_async_remote_copy(
        src_ref=others,
        dst_ref=others,
        send_sem=one_s,
        recv_sem=one_r,
        device_id=(in_plane(1), h),
        device_id_type=MESH,
    )
    all_ones.wait_recv()
    units = unit[...].reshape(PLANE * 16, HEAD_DIM)
    r, c = iota((ROWS, PLANE * 16), 0), iota((ROWS, PLANE * 16), 1)
    at = (r // HERE) * 16 + r % HERE
    pick_k = jnp.where(c == at, 1.0, 0.0).astype(BF)
    pick_v = jnp.where(c == at + HERE, 1.0, 0.0).astype(BF)
    coarse[plane_rows(z), 0:HEAD_DIM] = mm(pick_k, units).astype(BF)
    coarse[plane_rows(z), HEAD_DIM : 2 * HEAD_DIM] = mm(pick_v, units).astype(BF)

    def start_two(k, carry):
        two(k, z).start()
        return carry

    low = jnp.where(y == 1, 0, z)
    lax.fori_loop(low, z, start_two, 0)
    above = half + Z // 2 - 1 - z
    pl.when(above > 0)(lambda: pl.semaphore_wait(ready_near, above))
    lax.fori_loop(z + 1, half + Z // 2, start_two, 0)

    def send_far():
        pl.semaphore_wait(ready_far, Z // 2)
        lax.fori_loop(Z // 2, Z, start_two, 0)

    first = early & (y == 0) & (z < 2)
    pl.when(early & jnp.logical_not(first))(send_far)
    tail, _ = halo(3)
    pl.when(s + 1 < devices)(tail.start)
    for n in range(4):
        copy, step = halo(n)
        pl.when(s >= step)(copy.wait_recv)

    def got_two(k, carry):
        two(z, k).wait_recv()
        return carry

    lax.fori_loop(0, z, got_two, 0)
    lax.fori_loop(z + 1, jnp.where(y == 1, Z, z + 1), got_two, 0)
    for i in range(HERE):
        q_load(i).wait()

    wide = UNROLL * HEAD_DIM
    halves = qb.shape[2] // wide

    def sent(i, g):
        return pltpu.make_async_remote_copy(
            src_ref=ob.at[i, :, pl.ds(pl.multiple_of(g * wide, wide), wide)],
            dst_ref=out.at[:, pl.ds(pl.multiple_of(h * qb.shape[2] + g * wide, wide), wide)],
            send_sem=out_s.at[i, g],
            recv_sem=out_r.at[i, g],
            device_id=(s, target(i)),
            device_id_type=MESH,
        )

    def kept(g):
        return pltpu.make_async_copy(
            ob.at[3, :, pl.ds(pl.multiple_of(g * wide, wide), wide)],
            out.at[:, pl.ds(pl.multiple_of(h * qb.shape[2] + g * wide, wide), wide)],
            out_s.at[3, g],
        )

    causal = iota((BLK, BLK), 1) <= iota((BLK, BLK), 0)

    def step(t, carry):
        i, g = t // halves, t % halves
        j = target(i)
        block = s * HERE + j
        r0 = pl.multiple_of(j * BLK, BLK)
        m0 = pl.multiple_of(j * PER, PER)
        before = jnp.where(block >= 1, 0.0, -jnp.inf)
        mid_bias = jnp.where((block - 1 - MIDB) * PER + iota((1, MIDS), 1) >= 0, 0.0, -jnp.inf)
        p = iota((1, coarse.shape[0]), 1)
        c = (p // (X * HERE)) % Y * (Z * X * HERE) + p // ROWS * (X * HERE) + p % (X * HERE)
        coarse_bias = jnp.where(c <= block - MIDB - 2, 0.0, -jnp.inf)
        for u in range(UNROLL):
            col = pl.multiple_of((g * UNROLL + u) * HEAD_DIM, HEAD_DIM)
            q = qb[i, :, pl.ds(col, HEAD_DIM)]
            s1 = nt(q, near[pl.ds(r0, BLK), 0:HEAD_DIM]) + before
            s2 = nt(q, near[pl.ds(r0 + BLK, BLK), 0:HEAD_DIM])
            s2 = jnp.where(causal, s2, -jnp.inf)
            s3 = nt(q, mid[pl.ds(m0, MIDS), 0:HEAD_DIM]) + mid_bias
            s4 = nt(q, coarse[:, 0:HEAD_DIM]) + coarse_bias
            top = jnp.maximum(jnp.maximum(s1, s2), jnp.maximum(s3, s4))
            top = jnp.max(top, axis=1, keepdims=True) * SCALE
            p1, p2, p3, p4 = [jnp.exp2(x * SCALE - top).astype(BF) for x in (s1, s2, s3, s4)]
            o = mm(p1, near[pl.ds(r0, BLK), HEAD_DIM:]) + mm(p2, near[pl.ds(r0 + BLK, BLK), HEAD_DIM:])
            o = o + mm(p3, mid[pl.ds(m0, MIDS), HEAD_DIM:]) + mm(p4, coarse[:, HEAD_DIM:])
            ob[i, :, pl.ds(col, HEAD_DIM)] = (o[:, :HEAD_DIM] / o[:, HEAD_DIM:]).astype(BF)

        @pl.when(i < 3)
        def _():
            sent(i, g).start()

        @pl.when(i == 3)
        def _():
            kept(g).start()

        pl.when((t == 0) & first)(send_far)
        return carry

    lax.fori_loop(0, HERE * halves, step, 0)

    for n in range(4):
        copy, step_up = halo(n)
        pl.when(s + step_up < devices)(copy.wait_send)

    def sent_two(k, carry):
        two(k, z).wait_send()
        return carry

    lax.fori_loop(low, z, sent_two, 0)
    lax.fori_loop(z + 1, Z, sent_two, 0)
    all_ones.wait_send()
    for g in range(halves):
        for i in range(3):
            sent(i, g).wait()
        kept(g).wait()


def body(queries, keys, values, mid_pool, coarse_pool):
    rows, columns = queries.shape
    devices = lax.axis_size("seq")
    halves = columns // (UNROLL * HEAD_DIM)
    dma = pltpu.SemaphoreType.DMA
    hbm, any_ = pl.BlockSpec(memory_space=pltpu.HBM), pl.BlockSpec(memory_space=pl.ANY)
    return pl.pallas_call(
        kernel,
        out_shape=jax.ShapeDtypeStruct((rows // HERE, HERE * columns), BF),
        in_specs=[hbm] * 5,
        out_specs=any_,
        scratch_shapes=[
            pltpu.VMEM((HERE, BLK, columns), BF),
            pltpu.VMEM((HERE, BLK, columns), BF),
            pltpu.VMEM(((HERE + 1) * BLK, 384), BF),
            pltpu.VMEM((HERE * PER, 256), BF),
            pltpu.VMEM((352, 384), BF),
            pltpu.VMEM((devices * HERE, 384), BF),
            pltpu.VMEM((PLANE, 16, HEAD_DIM), BF),
            pltpu.VMEM((1, GROUP), BF),
            pltpu.VMEM((1, BLK), BF),
            dma((4,)),
            dma((HERE,)),
            dma((4,)),
            dma((4,)),
            dma,
            dma,
            dma((Z,)),
            dma((Z,)),
            pltpu.SemaphoreType.REGULAR,
            pltpu.SemaphoreType.REGULAR,
            dma((4, halves)),
            dma((3, halves)),
        ],
        compiler_params=pltpu.CompilerParams(
            collective_id=0, has_side_effects=True, vmem_limit_bytes=60 * 2**20
        ),
    )(queries, keys, values, mid_pool, coarse_pool)


def solution(mesh):
    return jax.shard_map(
        body,
        mesh=mesh,
        in_specs=(
            P("seq", "head"),
            P("seq", "head"),
            P("seq", "head"),
            P("head", None),
            P("head", None),
        ),
        out_specs=P(("seq", "head"), None),
        check_vma=False,
    )
```

```python
import math

import jax
import jax.numpy as jnp
from jax import lax
from jax.experimental import pallas as pl
from jax.experimental.pallas import tpu as pltpu
from jax.sharding import PartitionSpec as P

HEAD_DIM = 128
BLK = 256
GROUP = 8
PER = BLK // GROUP
MIDB = 8
MIDS = 256
HERE = 4
X, Z, Y = 4, 8, 2
PLANE = X * Y
ROWS = PLANE * HERE
UNROLL = 4
MESH = pl.DeviceIdType.MESH
BF = jnp.bfloat16
F32 = jnp.float32
SCALE = math.log2(math.e) / math.sqrt(HEAD_DIM)


def nt(a, b):
    return lax.dot_general(a, b, (((1,), (1,)), ((), ())), preferred_element_type=F32)


def mm(a, b):
    return jnp.dot(a, b, preferred_element_type=F32)


def iota(shape, dim):
    return lax.broadcasted_iota(jnp.int32, shape, dim)


def pool_matrix(mid_ref, coarse_ref):
    row, col = iota((48, BLK), 0), iota((48, BLK), 1)
    mids = mid_ref[...].astype(F32)
    spread = jnp.zeros((1, BLK), F32)
    lane = iota((1, BLK), 1) % GROUP
    for t in range(GROUP):
        spread = jnp.where(lane == t, mids[0:1, t : t + 1], spread)
    w = jnp.where((row < PER) & (col // GROUP == row), spread, 0.0)
    return jnp.where(row == PER, coarse_ref[...].astype(F32), w).astype(BF)


def kernel(
    queries,
    keys,
    values,
    mid_pool,
    coarse_pool,
    out,
    qb,
    ob,
    near,
    mymid,
    mid,
    coarse,
    unit,
    mid_w,
    coarse_w,
    in_sem,
    q_sem,
    halo_s,
    halo_r,
    one_s,
    one_r,
    two_s,
    two_r,
    ready_near,
    ready_far,
    ctx_s,
    ctx_r,
    out_s,
    out_r,
):
    s, h = lax.axis_index("seq"), lax.axis_index("head")
    devices = lax.axis_size("seq")
    y, z, x = s // (Z * X), (s // X) % Z, s % X
    u = y * X + x
    yh, core = h // 2, h % 2
    early = z < Z // 2

    def in_plane(i):
        v = (u + i) % PLANE
        return (v // X) * (Z * X) + z * X + v % X

    def at_z(k):
        return (y * Z + k) * X + x

    gives = (core == 1) & (y == 1)
    partner = h + 2 - 4 * yh

    def block_of(i):
        n = jnp.where(y == 1, jnp.where(i == 3, 3, (i + 2) % 3), i)
        there, here = (1 - yh) * 2 + (1 - n % 2), yh * 2 + (core + n + 1) % 2
        return jnp.where(gives, yh * 2 + i % 2, jnp.where(n < 2, there, here))

    def context_of(i):
        return jnp.where(gives, i // 2, 0)

    def heads_of(i):
        return jnp.where(gives & (i >= 2), partner, h)

    loads = [
        pltpu.make_async_copy(keys, near.at[0, pl.ds(BLK, HERE * BLK), pl.ds(0, HEAD_DIM)], in_sem.at[0]),
        pltpu.make_async_copy(
            values, near.at[0, pl.ds(BLK, HERE * BLK), pl.ds(HEAD_DIM, HEAD_DIM)], in_sem.at[1]
        ),
        pltpu.make_async_copy(mid_pool, mid_w, in_sem.at[2]),
        pltpu.make_async_copy(coarse_pool, coarse_w, in_sem.at[3]),
    ]
    for c in loads:
        c.start()

    def q_load(i):
        return pltpu.make_async_copy(
            queries.at[pl.ds(pl.multiple_of(block_of(i) * BLK, BLK), BLK)], qb.at[i], q_sem.at[i]
        )

    barrier = pltpu.get_barrier_semaphore()

    def tell(seq, head):
        pl.semaphore_signal(barrier, inc=1, device_id=(seq, head), device_id_type=MESH)

    for i in range(1, 4):
        tell(s, (h + i) % 4)
    for i in range(1, PLANE):
        tell(in_plane(i), h)
    for back in (1, 2, 3):

        @pl.when(s >= back)
        def _():
            tell(s - back, h)

    def tell_upper(k, carry):
        tell(at_z(k), h)
        return carry

    lax.fori_loop(z + 1, Z, tell_upper, 0)

    def blank(ref, start, size):
        ref[0, pl.ds(start, size), 0 : 2 * HEAD_DIM] = jnp.zeros((size, 2 * HEAD_DIM), BF)

    pl.when(s < 1)(lambda: blank(near, 0, BLK))
    pl.when(s < 1)(lambda: blank(mid, 160, 128))
    pl.when(s < 2)(lambda: blank(mid, 32, 128))
    pl.when(s < 3)(lambda: blank(mid, 0, 32))

    def blank_coarse(k, carry):
        blank(coarse, pl.multiple_of(k * ROWS, ROWS), ROWS)
        return carry

    lax.fori_loop(jnp.where(y == 0, z + 1, Z), Z, blank_coarse, 0)

    for ref in (near, mid, coarse):
        for k in range(2):
            ref[k, :, 2 * HEAD_DIM :] = jnp.ones((ref.shape[1], HEAD_DIM), BF)
    for c in loads:
        c.wait()
    for i in range(HERE):
        pl.when(jnp.logical_not(gives) | (i < 2))(q_load(i).start)
    pooling = pool_matrix(mid_w, coarse_w)
    tops = []
    for j in range(HERE):
        pooled = mm(pooling, near[0, BLK + j * BLK : 2 * BLK + j * BLK, 0 : 2 * HEAD_DIM])
        mymid[j * PER : (j + 1) * PER, :] = pooled[0:PER].astype(BF)
        if j < 2:
            mid[0, 288 + j * PER : 288 + (j + 1) * PER, 0 : 2 * HEAD_DIM] = pooled[0:PER].astype(BF)
        tops.append(pooled[PER : PER + 1])
    rows = [t[:, :HEAD_DIM] for t in tops] + [t[:, HEAD_DIM:] for t in tops]
    mine = jnp.zeros((16, HEAD_DIM), F32)
    for n, r in enumerate(rows):
        mine = jnp.where(iota((16, HEAD_DIM), 0) == n, r, mine)
    unit[u] = mine.astype(BF)

    pl.semaphore_wait(barrier, 3 + (PLANE - 1) + z + jnp.minimum(3, devices - 1 - s))

    half = z - z % (Z // 2)

    def tell_ready(sem):
        def tell_one(k, carry):
            pl.semaphore_signal(sem, inc=1, device_id=(at_z(k), h), device_id_type=MESH)
            return carry

        return tell_one

    lax.fori_loop(half, z, tell_ready(ready_near), 0)
    lax.fori_loop(0, half, tell_ready(ready_far), 0)

    def one(i):
        return pltpu.make_async_remote_copy(
            src_ref=unit.at[u],
            dst_ref=unit.at[u],
            send_sem=one_s,
            recv_sem=one_r,
            device_id=(in_plane(i), h),
            device_id_type=MESH,
        )

    def halo(n):
        src, dst, step = (
            (mymid, mid.at[0, pl.ds(160, 128), pl.ds(0, 256)], 1),
            (mymid, mid.at[0, pl.ds(32, 128), pl.ds(0, 256)], 2),
            (mymid.at[pl.ds(96, 32)], mid.at[0, pl.ds(0, 32), pl.ds(0, 256)], 3),
            (
                near.at[0, pl.ds(HERE * BLK, BLK), pl.ds(0, 256)],
                near.at[0, pl.ds(0, BLK), pl.ds(0, 256)],
                1,
            ),
        )[n]
        copy = pltpu.make_async_remote_copy(
            src_ref=src,
            dst_ref=dst,
            send_sem=halo_s.at[n],
            recv_sem=halo_r.at[n],
            device_id=(s + step, h),
            device_id_type=MESH,
        )
        return copy, step

    def give(n):
        away = 1 - yh
        even = pl.multiple_of(away * 2 * BLK, 2 * BLK)
        src, dst = (
            (queries.at[pl.ds(even, BLK)], qb.at[2]),
            (queries.at[pl.ds(even + BLK, BLK)], qb.at[3]),
            tuple(near.at[k, pl.ds(even + BLK, 2 * BLK), pl.ds(0, 256)] for k in (0, 1)),
            tuple(near.at[k, pl.ds(even, BLK), pl.ds(0, 256)] for k in (0, 1)),
            tuple(mid.at[k, pl.ds(pl.multiple_of(away * 64, 64), 288), pl.ds(0, 256)] for k in (0, 1)),
            tuple(coarse.at[k, :, pl.ds(0, 256)] for k in (0, 1)),
        )[n]
        return pltpu.make_async_remote_copy(
            src_ref=src,
            dst_ref=dst,
            send_sem=ctx_s.at[n],
            recv_sem=ctx_r.at[n],
            device_id=(s, partner),
            device_id_type=MESH,
        )

    def plane_rows(k):
        return pl.ds(pl.multiple_of(k * ROWS, ROWS), ROWS)

    def two(k, of):
        block = coarse.at[0, plane_rows(of), pl.ds(0, 256)]
        return pltpu.make_async_remote_copy(
            src_ref=block,
            dst_ref=block,
            send_sem=two_s.at[k],
            recv_sem=two_r.at[of],
            device_id=(at_z(k), h),
            device_id_type=MESH,
        )

    for i in range(1, PLANE):
        one(i).start()
    for n in range(3):
        copy, step = halo(n)
        pl.when(s + step < devices)(copy.start)
    for n in (2, 0, 1):
        pl.when(gives)(give(n).start)
    others = unit.at[pl.ds(0, PLANE - 1)]
    all_ones = pltpu.make_async_remote_copy(
        src_ref=others,
        dst_ref=others,
        send_sem=one_s,
        recv_sem=one_r,
        device_id=(in_plane(1), h),
        device_id_type=MESH,
    )
    all_ones.wait_recv()
    units = unit[...].reshape(PLANE * 16, HEAD_DIM)
    r, c = iota((ROWS, PLANE * 16), 0), iota((ROWS, PLANE * 16), 1)
    at = (r // HERE) * 16 + r % HERE
    pick_k = jnp.where(c == at, 1.0, 0.0).astype(BF)
    pick_v = jnp.where(c == at + HERE, 1.0, 0.0).astype(BF)
    coarse[0, plane_rows(z), 0:HEAD_DIM] = mm(pick_k, units).astype(BF)
    coarse[0, plane_rows(z), HEAD_DIM : 2 * HEAD_DIM] = mm(pick_v, units).astype(BF)

    def start_two(k, carry):
        two(k, z).start()
        return carry

    low = jnp.where(y == 1, 0, z)
    lax.fori_loop(low, z, start_two, 0)
    above = half + Z // 2 - 1 - z
    pl.when(above > 0)(lambda: pl.semaphore_wait(ready_near, above))
    lax.fori_loop(z + 1, half + Z // 2, start_two, 0)

    def send_far():
        pl.semaphore_wait(ready_far, Z // 2)
        lax.fori_loop(Z // 2, Z, start_two, 0)

    first = early & (y == 0) & (z < 2)
    pl.when(early & jnp.logical_not(first))(send_far)
    tail, _ = halo(3)
    pl.when(s + 1 < devices)(tail.start)
    for n in range(3):
        copy, step = halo(n)
        pl.when(s >= step)(copy.wait_recv)

    def got_two(k, carry):
        two(z, k).wait_recv()
        return carry

    lax.fori_loop(0, z, got_two, 0)
    lax.fori_loop(z + 1, jnp.where(y == 1, Z, z + 1), got_two, 0)
    for i in range(HERE):
        pl.when(jnp.logical_not(gives) | (i < 2))(q_load(i).wait)
    pl.when(gives & (s >= 1))(tail.wait_recv)
    for n in (4, 5, 3):
        pl.when(gives)(give(n).start)

    wide = UNROLL * HEAD_DIM
    halves = qb.shape[2] // wide

    def columns_of(head, g):
        return pl.ds(pl.multiple_of(head * qb.shape[2] + g * wide, wide), wide)

    def sent(i, g):
        return pltpu.make_async_remote_copy(
            src_ref=ob.at[i, :, pl.ds(pl.multiple_of(g * wide, wide), wide)],
            dst_ref=out.at[:, columns_of(heads_of(i), g)],
            send_sem=out_s.at[i, g],
            recv_sem=out_r.at[heads_of(i), g],
            device_id=(s, block_of(i)),
            device_id_type=MESH,
        )

    def arriving(source, g):
        block = out.at[:, columns_of(source, g)]
        return pltpu.make_async_remote_copy(
            src_ref=block,
            dst_ref=block,
            send_sem=out_s.at[0, g],
            recv_sem=out_r.at[source, g],
            device_id=(s, source),
            device_id_type=MESH,
        )

    def kept(i, g):
        return pltpu.make_async_copy(
            ob.at[i, :, pl.ds(pl.multiple_of(g * wide, wide), wide)],
            out.at[:, columns_of(heads_of(i), g)],
            out_s.at[i, g],
        )

    causal = iota((BLK, BLK), 1) <= iota((BLK, BLK), 0)

    def step(t, carry):
        i, g = t // halves, t % halves
        j, k = block_of(i), context_of(i)
        block = s * HERE + j
        pl.when((j == 0) & (g == 0) & (s >= 1) & jnp.logical_not(gives))(tail.wait_recv)

        @pl.when(gives & (t == 2 * halves))
        def _():
            for n in range(6):
                give(n).wait_recv()

        r0 = pl.multiple_of(j * BLK, BLK)
        m0 = pl.multiple_of(j * PER, PER)
        before = jnp.where(block >= 1, 0.0, -jnp.inf)
        mid_bias = jnp.where((block - 1 - MIDB) * PER + iota((1, MIDS), 1) >= 0, 0.0, -jnp.inf)
        p = iota((1, coarse.shape[1]), 1)
        c = (p // (X * HERE)) % Y * (Z * X * HERE) + p // ROWS * (X * HERE) + p % (X * HERE)
        coarse_bias = jnp.where(c <= block - MIDB - 2, 0.0, -jnp.inf)
        for u in range(UNROLL):
            col = pl.multiple_of((g * UNROLL + u) * HEAD_DIM, HEAD_DIM)
            q = qb[i, :, pl.ds(col, HEAD_DIM)]
            s1 = nt(q, near[k, pl.ds(r0, BLK), 0:HEAD_DIM]) + before
            s2 = nt(q, near[k, pl.ds(r0 + BLK, BLK), 0:HEAD_DIM])
            s2 = jnp.where(causal, s2, -jnp.inf)
            s3 = nt(q, mid[k, pl.ds(m0, MIDS), 0:HEAD_DIM]) + mid_bias
            s4 = nt(q, coarse[k, :, 0:HEAD_DIM]) + coarse_bias
            top = jnp.maximum(jnp.maximum(s1, s2), jnp.maximum(s3, s4))
            top = jnp.max(top, axis=1, keepdims=True) * SCALE
            p1, p2, p3, p4 = [jnp.exp2(x * SCALE - top).astype(BF) for x in (s1, s2, s3, s4)]
            o = mm(p1, near[k, pl.ds(r0, BLK), HEAD_DIM:]) + mm(p2, near[k, pl.ds(r0 + BLK, BLK), HEAD_DIM:])
            o = o + mm(p3, mid[k, pl.ds(m0, MIDS), HEAD_DIM:]) + mm(p4, coarse[k, :, HEAD_DIM:])
            ob[i, :, pl.ds(col, HEAD_DIM)] = (o[:, :HEAD_DIM] / o[:, HEAD_DIM:]).astype(BF)

        @pl.when(j != h)
        def _():
            sent(i, g).start()

        @pl.when(j == h)
        def _():
            kept(i, g).start()

        pl.when((t == 0) & first)(send_far)
        return carry

    lax.fori_loop(0, HERE * halves, step, 0)

    for n in range(4):
        copy, step_up = halo(n)
        pl.when(s + step_up < devices)(copy.wait_send)

    def sent_two(k, carry):
        two(k, z).wait_send()
        return carry

    lax.fori_loop(low, z, sent_two, 0)
    lax.fori_loop(z + 1, Z, sent_two, 0)
    all_ones.wait_send()
    for n in range(6):
        pl.when(gives)(give(n).wait_send)
    for g in range(halves):
        for i in range(HERE):
            pl.when(block_of(i) != h)(sent(i, g).wait_send)
            pl.when(block_of(i) == h)(kept(i, g).wait)
        for d in (1, 2, 3):
            other = (h + d) % 4
            pl.when(jnp.logical_not(gives) | (d != 2))(arriving(other, g).wait_recv)


def settle(src, dst, buf, sem):
    n, rows = 16, src.shape[0] // 16
    parts = [pl.ds(i * rows, rows) for i in range(n)]
    ins = [pltpu.make_async_copy(src.at[p], buf.at[p], sem.at[0, i]) for i, p in enumerate(parts)]
    outs = [pltpu.make_async_copy(buf.at[p], dst.at[p], sem.at[1, i]) for i, p in enumerate(parts)]
    for c in ins:
        c.start()
    for a, b in zip(ins, outs):
        a.wait()
        b.start()
    for b in outs:
        b.wait()


def body(queries, keys, values, mid_pool, coarse_pool):
    rows, columns = queries.shape
    devices = lax.axis_size("seq")
    halves = columns // (UNROLL * HEAD_DIM)
    dma = pltpu.SemaphoreType.DMA
    hbm, any_ = pl.BlockSpec(memory_space=pltpu.HBM), pl.BlockSpec(memory_space=pl.ANY)
    landed = pl.pallas_call(
        kernel,
        out_shape=jax.ShapeDtypeStruct((rows // HERE, HERE * columns), BF),
        in_specs=[hbm] * 5,
        out_specs=any_,
        scratch_shapes=[
            pltpu.VMEM((HERE, BLK, columns), BF),
            pltpu.VMEM((HERE, BLK, columns), BF),
            pltpu.VMEM((2, (HERE + 1) * BLK, 384), BF),
            pltpu.VMEM((HERE * PER, 256), BF),
            pltpu.VMEM((2, 352, 384), BF),
            pltpu.VMEM((2, devices * HERE, 384), BF),
            pltpu.VMEM((PLANE, 16, HEAD_DIM), BF),
            pltpu.VMEM((1, GROUP), BF),
            pltpu.VMEM((1, BLK), BF),
            dma((4,)),
            dma((HERE,)),
            dma((4,)),
            dma((4,)),
            dma,
            dma,
            dma((Z,)),
            dma((Z,)),
            pltpu.SemaphoreType.REGULAR,
            pltpu.SemaphoreType.REGULAR,
            dma((6,)),
            dma((6,)),
            dma((HERE, halves)),
            dma((4, halves)),
        ],
        compiler_params=pltpu.CompilerParams(
            collective_id=0, has_side_effects=True, vmem_limit_bytes=60 * 2**20
        ),
    )(queries, keys, values, mid_pool, coarse_pool)
    return pl.pallas_call(
        settle,
        out_shape=jax.ShapeDtypeStruct(landed.shape, BF),
        in_specs=[any_],
        out_specs=any_,
        scratch_shapes=[pltpu.VMEM(landed.shape, BF), dma((2, 16))],
        compiler_params=pltpu.CompilerParams(vmem_limit_bytes=60 * 2**20),
    )(landed)


def solution(mesh):
    return jax.shard_map(
        body,
        mesh=mesh,
        in_specs=(
            P("seq", "head"),
            P("seq", "head"),
            P("seq", "head"),
            P("head", None),
            P("head", None),
        ),
        out_specs=P(("seq", "head"), None),
        check_vma=False,
    )
```

```python
import math

import jax
import jax.numpy as jnp
from jax import lax
from jax.experimental import pallas as pl
from jax.experimental.pallas import tpu as pltpu
from jax.sharding import PartitionSpec as P

HEAD_DIM = 128
BLK = 256
GROUP = 8
PER = BLK // GROUP
MIDB = 8
MIDS = 256
HERE = 4
X, Z, Y = 4, 8, 2
PLANE = X * Y
ROWS = PLANE * HERE
UNROLL = 4
MESH = pl.DeviceIdType.MESH
BF = jnp.bfloat16
F32 = jnp.float32
SCALE = math.log2(math.e) / math.sqrt(HEAD_DIM)


def nt(a, b):
    return lax.dot_general(a, b, (((1,), (1,)), ((), ())), preferred_element_type=F32)


def mm(a, b):
    return jnp.dot(a, b, preferred_element_type=F32)


def iota(shape, dim):
    return lax.broadcasted_iota(jnp.int32, shape, dim)


def pool_matrix(mid_ref, coarse_ref):
    row, col = iota((48, BLK), 0), iota((48, BLK), 1)
    mids = mid_ref[...].astype(F32)
    spread = jnp.zeros((1, BLK), F32)
    lane = iota((1, BLK), 1) % GROUP
    for t in range(GROUP):
        spread = jnp.where(lane == t, mids[0:1, t : t + 1], spread)
    w = jnp.where((row < PER) & (col // GROUP == row), spread, 0.0)
    return jnp.where(row == PER, coarse_ref[...].astype(F32), w).astype(BF)


def kernel(
    queries,
    keys,
    values,
    mid_pool,
    coarse_pool,
    out,
    qb,
    ob,
    half_o,
    half_m,
    near,
    mymid,
    mid,
    coarse,
    unit,
    mid_w,
    coarse_w,
    in_sem,
    q_sem,
    halo_s,
    halo_r,
    one_s,
    one_r,
    two_s,
    two_r,
    ready_near,
    ready_far,
    ctx_s,
    ctx_r,
    out_s,
    out_r,
):
    s, h = lax.axis_index("seq"), lax.axis_index("head")
    devices = lax.axis_size("seq")
    y, z, x = s // (Z * X), (s // X) % Z, s % X
    u = y * X + x
    yh, core = h // 2, h % 2
    early = z < Z // 2

    def in_plane(i):
        v = (u + i) % PLANE
        return (v // X) * (Z * X) + z * X + v % X

    def at_z(k):
        return (y * Z + k) * X + x

    gives = (core == 1) & (s > 0)
    both = gives & (y == 1)
    taken = jnp.where(gives, 3 - y, HERE)
    partner = h + 2 - 4 * yh

    def block_of(i):
        odd, even = (1 - yh) * 2 + 1, (1 - yh) * 2
        other, own = yh * 2 + 1 - core, yh * 2 + core

        def pick(*blocks):
            return jnp.where(i == 0, blocks[0], jnp.where(i == 1, blocks[1], jnp.where(i == 2, blocks[2], blocks[3])))

        giving = jnp.where(y == 1, pick(own, other, other, own), pick(odd, other, own, other))
        return jnp.where(gives, giving, jnp.where(y == 1, pick(other, odd, even, own), pick(odd, even, other, own)))

    def context_of(i):
        return jnp.where(i >= taken, 1, 0)

    def heads_of(i):
        return jnp.where(i >= taken, partner, h)

    loads = [
        pltpu.make_async_copy(keys, near.at[0, pl.ds(BLK, HERE * BLK), pl.ds(0, HEAD_DIM)], in_sem.at[0]),
        pltpu.make_async_copy(
            values, near.at[0, pl.ds(BLK, HERE * BLK), pl.ds(HEAD_DIM, HEAD_DIM)], in_sem.at[1]
        ),
        pltpu.make_async_copy(mid_pool, mid_w, in_sem.at[2]),
        pltpu.make_async_copy(coarse_pool, coarse_w, in_sem.at[3]),
    ]
    for c in loads:
        c.start()

    def q_load(i):
        return pltpu.make_async_copy(
            queries.at[pl.ds(pl.multiple_of(block_of(i) * BLK, BLK), BLK)], qb.at[i], q_sem.at[i]
        )

    barrier = pltpu.get_barrier_semaphore()

    def tell(seq, head):
        pl.semaphore_signal(barrier, inc=1, device_id=(seq, head), device_id_type=MESH)

    for i in range(1, 4):
        tell(s, (h + i) % 4)
    for i in range(1, PLANE):
        tell(in_plane(i), h)
    for back in (1, 2, 3):

        @pl.when(s >= back)
        def _():
            tell(s - back, h)

    def tell_upper(k, carry):
        tell(at_z(k), h)
        return carry

    lax.fori_loop(z + 1, Z, tell_upper, 0)

    def blank(ref, start, size):
        ref[0, pl.ds(start, size), 0 : 2 * HEAD_DIM] = jnp.zeros((size, 2 * HEAD_DIM), BF)

    pl.when(s < 1)(lambda: blank(near, 0, BLK))
    pl.when(s < 1)(lambda: blank(coarse, 0, ROWS))
    pl.when(s < 1)(lambda: blank(mid, 160, 128))
    pl.when(s < 2)(lambda: blank(mid, 32, 128))
    pl.when(s < 3)(lambda: blank(mid, 0, 32))

    def blank_coarse(k, carry):
        blank(coarse, pl.multiple_of(k * ROWS, ROWS), ROWS)
        return carry

    lax.fori_loop(jnp.where(y == 0, z + 1, Z), Z, blank_coarse, 0)

    for ref in (near, mid, coarse):
        for k in range(2):
            ref[k, :, 2 * HEAD_DIM :] = jnp.ones((ref.shape[1], HEAD_DIM), BF)
    for c in loads:
        c.wait()
    for i in range(HERE):
        pl.when(i < taken)(q_load(i).start)
    pooling = pool_matrix(mid_w, coarse_w)
    tops = []
    for j in range(HERE):
        pooled = mm(pooling, near[0, BLK + j * BLK : 2 * BLK + j * BLK, 0 : 2 * HEAD_DIM])
        mymid[j * PER : (j + 1) * PER, :] = pooled[0:PER].astype(BF)
        if j < 2:
            mid[0, 288 + j * PER : 288 + (j + 1) * PER, 0 : 2 * HEAD_DIM] = pooled[0:PER].astype(BF)
        tops.append(pooled[PER : PER + 1])
    rows = [t[:, :HEAD_DIM] for t in tops] + [t[:, HEAD_DIM:] for t in tops]
    mine = jnp.zeros((16, HEAD_DIM), F32)
    for n, r in enumerate(rows):
        mine = jnp.where(iota((16, HEAD_DIM), 0) == n, r, mine)
    unit[u] = mine.astype(BF)

    pl.semaphore_wait(barrier, 3 + (PLANE - 1) + z + jnp.minimum(3, devices - 1 - s))

    half = z - z % (Z // 2)

    def tell_ready(sem):
        def tell_one(k, carry):
            pl.semaphore_signal(sem, inc=1, device_id=(at_z(k), h), device_id_type=MESH)
            return carry

        return tell_one

    lax.fori_loop(half, z, tell_ready(ready_near), 0)
    lax.fori_loop(0, half, tell_ready(ready_far), 0)

    def one(i):
        return pltpu.make_async_remote_copy(
            src_ref=unit.at[u],
            dst_ref=unit.at[u],
            send_sem=one_s,
            recv_sem=one_r,
            device_id=(in_plane(i), h),
            device_id_type=MESH,
        )

    def halo(n):
        src, dst, step = (
            (mymid, mid.at[0, pl.ds(160, 128), pl.ds(0, 256)], 1),
            (mymid, mid.at[0, pl.ds(32, 128), pl.ds(0, 256)], 2),
            (mymid.at[pl.ds(96, 32)], mid.at[0, pl.ds(0, 32), pl.ds(0, 256)], 3),
            (
                near.at[0, pl.ds(HERE * BLK, BLK), pl.ds(0, 256)],
                near.at[0, pl.ds(0, BLK), pl.ds(0, 256)],
                1,
            ),
        )[n]
        copy = pltpu.make_async_remote_copy(
            src_ref=src,
            dst_ref=dst,
            send_sem=halo_s.at[n],
            recv_sem=halo_r.at[n],
            device_id=(s + step, h),
            device_id_type=MESH,
        )
        return copy, step

    def give(n):
        away = 1 - yh
        even = pl.multiple_of(away * 2 * BLK, 2 * BLK)
        src, dst = (
            (queries.at[pl.ds(even, BLK)], qb.at[jnp.where(both, 2, 3)]),
            (queries.at[pl.ds(even + BLK, BLK)], qb.at[3]),
            tuple(near.at[k, pl.ds(even + BLK, BLK), pl.ds(0, 256)] for k in (0, 1)),
            tuple(near.at[k, pl.ds(even, BLK), pl.ds(0, 256)] for k in (0, 1)),
            tuple(mid.at[k, pl.ds(pl.multiple_of(away * 64, 64), 288), pl.ds(0, 256)] for k in (0, 1)),
            tuple(coarse.at[k, :, pl.ds(0, 256)] for k in (0, 1)),
            tuple(near.at[k, pl.ds(even + 2 * BLK, BLK), pl.ds(0, 256)] for k in (0, 1)),
        )[n]
        return pltpu.make_async_remote_copy(
            src_ref=src,
            dst_ref=dst,
            send_sem=ctx_s.at[n],
            recv_sem=ctx_r.at[n],
            device_id=(s, partner),
            device_id_type=MESH,
        )

    def plane_rows(k):
        return pl.ds(pl.multiple_of(k * ROWS, ROWS), ROWS)

    def two(k, of):
        block = coarse.at[0, plane_rows(of), pl.ds(0, 256)]
        return pltpu.make_async_remote_copy(
            src_ref=block,
            dst_ref=block,
            send_sem=two_s.at[k],
            recv_sem=two_r.at[of],
            device_id=(at_z(k), h),
            device_id_type=MESH,
        )

    for i in range(1, PLANE):
        one(i).start()
    for n in range(3):
        copy, step = halo(n)
        pl.when(s + step < devices)(copy.start)
    tail, _ = halo(3)
    pl.when(s + 1 < devices)(tail.start)
    for n in (2, 0):
        pl.when(gives)(give(n).start)
    for n in (6, 1):
        pl.when(both)(give(n).start)
    def start_two(k, carry):
        two(k, z).start()
        return carry

    def send_far():
        pl.semaphore_wait(ready_far, Z // 2)
        lax.fori_loop(Z // 2, Z, start_two, 0)

    first = early & (y == 0) & (z < 2)
    causal = iota((BLK, BLK), 1) <= iota((BLK, BLK), 0)
    own0 = pl.multiple_of(block_of(0) * BLK, BLK)

    def near_step(g, carry):
        for u in range(UNROLL):
            col = pl.multiple_of((g * UNROLL + u) * HEAD_DIM, HEAD_DIM)
            col2 = pl.multiple_of((g * UNROLL + u) * 2 * HEAD_DIM, 2 * HEAD_DIM)
            q = qb[0, :, pl.ds(col, HEAD_DIM)]
            s1 = nt(q, near[0, pl.ds(own0, BLK), 0:HEAD_DIM])
            s2 = nt(q, near[0, pl.ds(own0 + BLK, BLK), 0:HEAD_DIM])
            s2 = jnp.where(causal, s2, -jnp.inf)
            top = jnp.max(jnp.maximum(s1, s2), axis=1, keepdims=True) * SCALE
            p1, p2 = [jnp.exp2(x * SCALE - top).astype(BF) for x in (s1, s2)]
            o = mm(p1, near[0, pl.ds(own0, BLK), HEAD_DIM:]) + mm(p2, near[0, pl.ds(own0 + BLK, BLK), HEAD_DIM:])
            half_o[:, pl.ds(col2, 2 * HEAD_DIM)] = o
            half_m[:, pl.ds(col, HEAD_DIM)] = jnp.broadcast_to(top, (BLK, HEAD_DIM))
        return carry

    wide = UNROLL * HEAD_DIM
    halves = qb.shape[2] // wide

    def columns_of(head, g):
        return pl.ds(pl.multiple_of(head * qb.shape[2] + g * wide, wide), wide)

    def sent(i, g):
        return pltpu.make_async_remote_copy(
            src_ref=ob.at[i, :, pl.ds(pl.multiple_of(g * wide, wide), wide)],
            dst_ref=out.at[:, columns_of(heads_of(i), g)],
            send_sem=out_s.at[i, g],
            recv_sem=out_r.at[heads_of(i), g],
            device_id=(s, block_of(i)),
            device_id_type=MESH,
        )

    def arriving(source, g):
        block = out.at[:, columns_of(source, g)]
        return pltpu.make_async_remote_copy(
            src_ref=block,
            dst_ref=block,
            send_sem=out_s.at[0, g],
            recv_sem=out_r.at[source, g],
            device_id=(s, source),
            device_id_type=MESH,
        )

    def kept(i, g):
        return pltpu.make_async_copy(
            ob.at[i, :, pl.ds(pl.multiple_of(g * wide, wide), wide)],
            out.at[:, columns_of(heads_of(i), g)],
            out_s.at[i, g],
        )

    def mid_bias_of(block):
        return jnp.where((block - 1 - MIDB) * PER + iota((1, MIDS), 1) >= 0, 0.0, -jnp.inf)

    def coarse_bias_of(block):
        p = iota((1, coarse.shape[1]), 1)
        c = (p // (X * HERE)) % Y * (Z * X * HERE) + p // ROWS * (X * HERE) + p % (X * HERE)
        return jnp.where(c <= block - MIDB - 2, 0.0, -jnp.inf)

    def deliver(i, g):
        @pl.when(block_of(i) != h)
        def _():
            sent(i, g).start()

        @pl.when(block_of(i) == h)
        def _():
            kept(i, g).start()

    def first_step(g, carry):
        block = s * HERE + block_of(0)
        m0 = pl.multiple_of(block_of(0) * PER, PER)
        mid_bias, coarse_bias = mid_bias_of(block), coarse_bias_of(block)
        for u in range(UNROLL):
            col = pl.multiple_of((g * UNROLL + u) * HEAD_DIM, HEAD_DIM)
            col2 = pl.multiple_of((g * UNROLL + u) * 2 * HEAD_DIM, 2 * HEAD_DIM)
            q = qb[0, :, pl.ds(col, HEAD_DIM)]
            s3 = nt(q, mid[0, pl.ds(m0, MIDS), 0:HEAD_DIM]) + mid_bias
            s4 = nt(q, coarse[0, :, 0:HEAD_DIM]) + coarse_bias
            before = half_m[:, pl.ds(col, HEAD_DIM)][:, 0:1]
            top = jnp.maximum(jnp.max(jnp.maximum(s3, s4), axis=1, keepdims=True) * SCALE, before)
            p3, p4 = [jnp.exp2(x * SCALE - top).astype(BF) for x in (s3, s4)]
            o = half_o[:, pl.ds(col2, 2 * HEAD_DIM)] * jnp.exp2(before - top)
            o = o + mm(p3, mid[0, pl.ds(m0, MIDS), HEAD_DIM:]) + mm(p4, coarse[0, :, HEAD_DIM:])
            ob[0, :, pl.ds(col, HEAD_DIM)] = (o[:, :HEAD_DIM] / o[:, HEAD_DIM:]).astype(BF)
        deliver(0, g)
        pl.when((g == 0) & first & (s > 0))(send_far)
        return carry

    def near_part():
        q_load(0).wait()
        lax.fori_loop(0, halves, near_step, 0)

    @pl.when(s == 0)
    def _():
        near_part()
        lax.fori_loop(0, halves, first_step, 0)

    others = unit.at[pl.ds(0, PLANE - 1)]
    all_ones = pltpu.make_async_remote_copy(
        src_ref=others,
        dst_ref=others,
        send_sem=one_s,
        recv_sem=one_r,
        device_id=(in_plane(1), h),
        device_id_type=MESH,
    )
    all_ones.wait_recv()
    units = unit[...].reshape(PLANE * 16, HEAD_DIM)
    r, c = iota((ROWS, PLANE * 16), 0), iota((ROWS, PLANE * 16), 1)
    at = (r // HERE) * 16 + r % HERE
    pick_k = jnp.where(c == at, 1.0, 0.0).astype(BF)
    pick_v = jnp.where(c == at + HERE, 1.0, 0.0).astype(BF)
    coarse[0, plane_rows(z), 0:HEAD_DIM] = mm(pick_k, units).astype(BF)
    coarse[0, plane_rows(z), HEAD_DIM : 2 * HEAD_DIM] = mm(pick_v, units).astype(BF)

    low = jnp.where(y == 1, 0, z)
    lax.fori_loop(low, z, start_two, 0)
    above = half + Z // 2 - 1 - z
    pl.when(above > 0)(lambda: pl.semaphore_wait(ready_near, above))
    lax.fori_loop(z + 1, half + Z // 2, start_two, 0)

    pl.when(early & jnp.logical_not(first))(send_far)

    pl.when(s > 0)(near_part)
    for n in range(3):
        copy, step = halo(n)
        pl.when(s >= step)(copy.wait_recv)

    def got_two(k, carry):
        two(z, k).wait_recv()
        return carry

    lax.fori_loop(0, z, got_two, 0)
    lax.fori_loop(z + 1, jnp.where(y == 1, Z, z + 1), got_two, 0)
    for i in range(1, HERE):
        pl.when(i < taken)(q_load(i).wait)
    for n in (4, 5):
        pl.when(gives)(give(n).start)
    pl.when(gives & (s >= 1))(tail.wait_recv)
    pl.when(gives)(give(3).start)

    @pl.when(s > 0)
    def _():
        lax.fori_loop(0, halves, first_step, 0)

    pl.when(s == 0)(send_far)

    def step(t, carry):
        i, g = t // halves, t % halves
        j, k = block_of(i), context_of(i)
        block = s * HERE + j
        pl.when((j == 0) & (g == 0) & (s >= 1) & jnp.logical_not(gives))(tail.wait_recv)

        @pl.when(t == taken * halves)
        def _():
            for n in (0, 2, 3, 4, 5):
                give(n).wait_recv()

        pl.when(both & (t == 2 * halves))(give(6).wait_recv)
        pl.when(both & (t == 3 * halves))(give(1).wait_recv)
        r0 = pl.multiple_of(j * BLK, BLK)
        m0 = pl.multiple_of(j * PER, PER)
        before = jnp.where(block >= 1, 0.0, -jnp.inf)
        mid_bias, coarse_bias = mid_bias_of(block), coarse_bias_of(block)
        for u in range(UNROLL):
            col = pl.multiple_of((g * UNROLL + u) * HEAD_DIM, HEAD_DIM)
            q = qb[i, :, pl.ds(col, HEAD_DIM)]
            s1 = nt(q, near[k, pl.ds(r0, BLK), 0:HEAD_DIM]) + before
            s2 = nt(q, near[k, pl.ds(r0 + BLK, BLK), 0:HEAD_DIM])
            s2 = jnp.where(causal, s2, -jnp.inf)
            s3 = nt(q, mid[k, pl.ds(m0, MIDS), 0:HEAD_DIM]) + mid_bias
            s4 = nt(q, coarse[k, :, 0:HEAD_DIM]) + coarse_bias
            top = jnp.maximum(jnp.maximum(s1, s2), jnp.maximum(s3, s4))
            top = jnp.max(top, axis=1, keepdims=True) * SCALE
            p1, p2, p3, p4 = [jnp.exp2(x * SCALE - top).astype(BF) for x in (s1, s2, s3, s4)]
            o = mm(p1, near[k, pl.ds(r0, BLK), HEAD_DIM:]) + mm(p2, near[k, pl.ds(r0 + BLK, BLK), HEAD_DIM:])
            o = o + mm(p3, mid[k, pl.ds(m0, MIDS), HEAD_DIM:]) + mm(p4, coarse[k, :, HEAD_DIM:])
            ob[i, :, pl.ds(col, HEAD_DIM)] = (o[:, :HEAD_DIM] / o[:, HEAD_DIM:]).astype(BF)

        deliver(i, g)
        return carry

    lax.fori_loop(halves, HERE * halves, step, 0)

    for n in range(4):
        copy, step_up = halo(n)
        pl.when(s + step_up < devices)(copy.wait_send)

    def sent_two(k, carry):
        two(k, z).wait_send()
        return carry

    lax.fori_loop(low, z, sent_two, 0)
    lax.fori_loop(z + 1, Z, sent_two, 0)
    all_ones.wait_send()
    for n in (0, 2, 3, 4, 5):
        pl.when(gives)(give(n).wait_send)
    for n in (1, 6):
        pl.when(both)(give(n).wait_send)
    for g in range(halves):
        for i in range(HERE):
            pl.when(block_of(i) != h)(sent(i, g).wait_send)
            pl.when(block_of(i) == h)(kept(i, g).wait)
        for d in (1, 2, 3):
            other = (h + d) % 4
            pl.when(jnp.logical_not(both) | (d != 2))(arriving(other, g).wait_recv)


def settle(src, dst, buf, sem):
    n, rows = 16, src.shape[0] // 16
    parts = [pl.ds(i * rows, rows) for i in range(n)]
    ins = [pltpu.make_async_copy(src.at[p], buf.at[p], sem.at[0, i]) for i, p in enumerate(parts)]
    outs = [pltpu.make_async_copy(buf.at[p], dst.at[p], sem.at[1, i]) for i, p in enumerate(parts)]
    for c in ins:
        c.start()
    for a, b in zip(ins, outs):
        a.wait()
        b.start()
    for b in outs:
        b.wait()


def body(queries, keys, values, mid_pool, coarse_pool):
    rows, columns = queries.shape
    devices = lax.axis_size("seq")
    halves = columns // (UNROLL * HEAD_DIM)
    dma = pltpu.SemaphoreType.DMA
    hbm, any_ = pl.BlockSpec(memory_space=pltpu.HBM), pl.BlockSpec(memory_space=pl.ANY)
    landed = pl.pallas_call(
        kernel,
        out_shape=jax.ShapeDtypeStruct((rows // HERE, HERE * columns), BF),
        in_specs=[hbm] * 5,
        out_specs=any_,
        scratch_shapes=[
            pltpu.VMEM((HERE, BLK, columns), BF),
            pltpu.VMEM((HERE, BLK, columns), BF),
            pltpu.VMEM((BLK, 2 * columns), F32),
            pltpu.VMEM((BLK, columns), F32),
            pltpu.VMEM((2, (HERE + 1) * BLK, 384), BF),
            pltpu.VMEM((HERE * PER, 256), BF),
            pltpu.VMEM((2, 352, 384), BF),
            pltpu.VMEM((2, devices * HERE, 384), BF),
            pltpu.VMEM((PLANE, 16, HEAD_DIM), BF),
            pltpu.VMEM((1, GROUP), BF),
            pltpu.VMEM((1, BLK), BF),
            dma((4,)),
            dma((HERE,)),
            dma((4,)),
            dma((4,)),
            dma,
            dma,
            dma((Z,)),
            dma((Z,)),
            pltpu.SemaphoreType.REGULAR,
            pltpu.SemaphoreType.REGULAR,
            dma((7,)),
            dma((7,)),
            dma((HERE, halves)),
            dma((4, halves)),
        ],
        compiler_params=pltpu.CompilerParams(
            collective_id=0, has_side_effects=True, vmem_limit_bytes=60 * 2**20
        ),
    )(queries, keys, values, mid_pool, coarse_pool)
    return pl.pallas_call(
        settle,
        out_shape=jax.ShapeDtypeStruct(landed.shape, BF),
        in_specs=[any_],
        out_specs=any_,
        scratch_shapes=[pltpu.VMEM(landed.shape, BF), dma((2, 16))],
        compiler_params=pltpu.CompilerParams(vmem_limit_bytes=60 * 2**20),
    )(landed)


def solution(mesh):
    return jax.shard_map(
        body,
        mesh=mesh,
        in_specs=(
            P("seq", "head"),
            P("seq", "head"),
            P("seq", "head"),
            P("head", None),
            P("head", None),
        ),
        out_specs=P(("seq", "head"), None),
        check_vma=False,
    )
```

```python
import math

import jax
import jax.numpy as jnp
from jax import lax
from jax.experimental import pallas as pl
from jax.experimental.pallas import tpu as pltpu
from jax.sharding import PartitionSpec as P

HEAD_DIM = 128
BLK = 256
GROUP = 8
PER = BLK // GROUP
MIDB = 8
MIDS = 256
HERE = 4
X, Z, Y = 4, 8, 2
PLANE = X * Y
ROWS = PLANE * HERE
UNROLL = 4
MESH = pl.DeviceIdType.MESH
BF = jnp.bfloat16
F32 = jnp.float32
SCALE = math.log2(math.e) / math.sqrt(HEAD_DIM)


def nt(a, b):
    return lax.dot_general(a, b, (((1,), (1,)), ((), ())), preferred_element_type=F32)


def mm(a, b):
    return jnp.dot(a, b, preferred_element_type=F32)


def iota(shape, dim):
    return lax.broadcasted_iota(jnp.int32, shape, dim)


def pool_matrix(mid_ref, coarse_ref):
    row, col = iota((48, BLK), 0), iota((48, BLK), 1)
    mids = mid_ref[...].astype(F32)
    spread = jnp.zeros((1, BLK), F32)
    lane = iota((1, BLK), 1) % GROUP
    for t in range(GROUP):
        spread = jnp.where(lane == t, mids[0:1, t : t + 1], spread)
    w = jnp.where((row < PER) & (col // GROUP == row), spread, 0.0)
    return jnp.where(row == PER, coarse_ref[...].astype(F32), w).astype(BF)


def kernel(
    queries,
    keys,
    values,
    mid_pool,
    coarse_pool,
    out,
    qb,
    ob,
    half_o,
    half_m,
    near,
    mymid,
    mid,
    coarse,
    unit,
    mid_w,
    coarse_w,
    in_sem,
    q_sem,
    halo_s,
    halo_r,
    one_s,
    one_r,
    two_s,
    two_r,
    ready_near,
    ready_far,
    ctx_s,
    ctx_r,
    out_s,
    out_r,
):
    s, h = lax.axis_index("seq"), lax.axis_index("head")
    devices = lax.axis_size("seq")
    y, z, x = s // (Z * X), (s // X) % Z, s % X
    u = y * X + x
    yh, core = h // 2, h % 2
    early = z < Z // 2

    def in_plane(i):
        v = (u + i) % PLANE
        return (v // X) * (Z * X) + z * X + v % X

    def at_z(k):
        return (y * Z + k) * X + x

    gives = (core == 1) & (s > 0)
    both = gives & (y == 1)
    taken = jnp.where(gives, 3 - y, HERE)
    partner = h + 2 - 4 * yh

    def block_of(i):
        odd, even = (1 - yh) * 2 + 1, (1 - yh) * 2
        other, own = yh * 2 + 1 - core, yh * 2 + core

        late = (y == 1) & (z >= 2)

        def pick(*blocks):
            return jnp.where(i == 0, blocks[0], jnp.where(i == 1, blocks[1], jnp.where(i == 2, blocks[2], blocks[3])))

        giving = jnp.where(y == 1, pick(own, other, other, own), pick(odd, other, own, other))
        return jnp.where(gives, giving, jnp.where(late, pick(other, odd, even, own), jnp.where(y == 1, pick(odd, other, even, own), pick(odd, even, other, own))))

    def context_of(i):
        return jnp.where(i >= taken, 1, 0)

    def heads_of(i):
        return jnp.where(i >= taken, partner, h)

    loads = [
        pltpu.make_async_copy(keys, near.at[0, pl.ds(BLK, HERE * BLK), pl.ds(0, HEAD_DIM)], in_sem.at[0]),
        pltpu.make_async_copy(
            values, near.at[0, pl.ds(BLK, HERE * BLK), pl.ds(HEAD_DIM, HEAD_DIM)], in_sem.at[1]
        ),
        pltpu.make_async_copy(mid_pool, mid_w, in_sem.at[2]),
        pltpu.make_async_copy(coarse_pool, coarse_w, in_sem.at[3]),
    ]
    for c in loads:
        c.start()

    def q_load(i):
        return pltpu.make_async_copy(
            queries.at[pl.ds(pl.multiple_of(block_of(i) * BLK, BLK), BLK)], qb.at[i], q_sem.at[i]
        )

    barrier = pltpu.get_barrier_semaphore()

    def tell(seq, head):
        pl.semaphore_signal(barrier, inc=1, device_id=(seq, head), device_id_type=MESH)

    for i in range(1, 4):
        tell(s, (h + i) % 4)
    for i in range(1, PLANE):
        tell(in_plane(i), h)
    for back in (1, 2, 3):

        @pl.when(s >= back)
        def _():
            tell(s - back, h)

    def tell_upper(k, carry):
        tell(at_z(k), h)
        return carry

    lax.fori_loop(z + 1, Z, tell_upper, 0)

    def blank(ref, start, size):
        ref[0, pl.ds(start, size), 0 : 2 * HEAD_DIM] = jnp.zeros((size, 2 * HEAD_DIM), BF)

    pl.when(s < 1)(lambda: blank(near, 0, BLK))
    pl.when(s < 1)(lambda: blank(coarse, 0, ROWS))
    pl.when(s < 1)(lambda: blank(mid, 160, 128))
    pl.when(s < 2)(lambda: blank(mid, 32, 128))
    pl.when(s < 3)(lambda: blank(mid, 0, 32))

    def blank_coarse(k, carry):
        blank(coarse, pl.multiple_of(k * ROWS, ROWS), ROWS)
        return carry

    lax.fori_loop(jnp.where(y == 0, z + 1, Z), Z, blank_coarse, 0)

    for ref in (near, mid, coarse):
        for k in range(2):
            ref[k, :, 2 * HEAD_DIM :] = jnp.ones((ref.shape[1], HEAD_DIM), BF)
    for c in loads:
        c.wait()
    for i in range(HERE):
        pl.when(i < taken)(q_load(i).start)
    pooling = pool_matrix(mid_w, coarse_w)
    tops = []
    for j in range(HERE):
        pooled = mm(pooling, near[0, BLK + j * BLK : 2 * BLK + j * BLK, 0 : 2 * HEAD_DIM])
        mymid[j * PER : (j + 1) * PER, :] = pooled[0:PER].astype(BF)
        if j < 2:
            mid[0, 288 + j * PER : 288 + (j + 1) * PER, 0 : 2 * HEAD_DIM] = pooled[0:PER].astype(BF)
        tops.append(pooled[PER : PER + 1])
    rows = [t[:, :HEAD_DIM] for t in tops] + [t[:, HEAD_DIM:] for t in tops]
    mine = jnp.zeros((16, HEAD_DIM), F32)
    for n, r in enumerate(rows):
        mine = jnp.where(iota((16, HEAD_DIM), 0) == n, r, mine)
    unit[u] = mine.astype(BF)

    pl.semaphore_wait(barrier, 3 + (PLANE - 1) + z + jnp.minimum(3, devices - 1 - s))

    half = z - z % (Z // 2)

    def tell_ready(sem):
        def tell_one(k, carry):
            pl.semaphore_signal(sem, inc=1, device_id=(at_z(k), h), device_id_type=MESH)
            return carry

        return tell_one

    lax.fori_loop(half, z, tell_ready(ready_near), 0)
    lax.fori_loop(0, half, tell_ready(ready_far), 0)

    def one(i):
        return pltpu.make_async_remote_copy(
            src_ref=unit.at[u],
            dst_ref=unit.at[u],
            send_sem=one_s,
            recv_sem=one_r,
            device_id=(in_plane(i), h),
            device_id_type=MESH,
        )

    def halo(n):
        src, dst, step = (
            (mymid, mid.at[0, pl.ds(160, 128), pl.ds(0, 256)], 1),
            (mymid, mid.at[0, pl.ds(32, 128), pl.ds(0, 256)], 2),
            (mymid.at[pl.ds(96, 32)], mid.at[0, pl.ds(0, 32), pl.ds(0, 256)], 3),
            (
                near.at[0, pl.ds(HERE * BLK, BLK), pl.ds(0, 256)],
                near.at[0, pl.ds(0, BLK), pl.ds(0, 256)],
                1,
            ),
        )[n]
        copy = pltpu.make_async_remote_copy(
            src_ref=src,
            dst_ref=dst,
            send_sem=halo_s.at[n],
            recv_sem=halo_r.at[n],
            device_id=(s + step, h),
            device_id_type=MESH,
        )
        return copy, step

    def give(n):
        away = 1 - yh
        even = pl.multiple_of(away * 2 * BLK, 2 * BLK)
        src, dst = (
            (queries.at[pl.ds(even, BLK)], qb.at[jnp.where(both, 2, 3)]),
            (queries.at[pl.ds(even + BLK, BLK)], qb.at[3]),
            tuple(near.at[k, pl.ds(even + BLK, BLK), pl.ds(0, 256)] for k in (0, 1)),
            tuple(near.at[k, pl.ds(even, BLK), pl.ds(0, 256)] for k in (0, 1)),
            tuple(mid.at[k, pl.ds(pl.multiple_of(away * 64, 64), 288), pl.ds(0, 256)] for k in (0, 1)),
            tuple(coarse.at[k, :, pl.ds(0, 256)] for k in (0, 1)),
            tuple(near.at[k, pl.ds(even + 2 * BLK, BLK), pl.ds(0, 256)] for k in (0, 1)),
        )[n]
        return pltpu.make_async_remote_copy(
            src_ref=src,
            dst_ref=dst,
            send_sem=ctx_s.at[n],
            recv_sem=ctx_r.at[n],
            device_id=(s, partner),
            device_id_type=MESH,
        )

    def plane_rows(k):
        return pl.ds(pl.multiple_of(k * ROWS, ROWS), ROWS)

    def two(k, of):
        block = coarse.at[0, plane_rows(of), pl.ds(0, 256)]
        return pltpu.make_async_remote_copy(
            src_ref=block,
            dst_ref=block,
            send_sem=two_s.at[k],
            recv_sem=two_r.at[of],
            device_id=(at_z(k), h),
            device_id_type=MESH,
        )

    for i in range(1, PLANE):
        one(i).start()
    for n in range(3):
        copy, step = halo(n)
        pl.when(s + step < devices)(copy.start)
    tail, _ = halo(3)
    pl.when(s + 1 < devices)(tail.start)
    for n in (2, 0):
        pl.when(gives)(give(n).start)
    for n in (6, 1):
        pl.when(both)(give(n).start)
    def start_two(k, carry):
        two(k, z).start()
        return carry

    def send_far():
        pl.semaphore_wait(ready_far, Z // 2)
        lax.fori_loop(Z // 2, Z, start_two, 0)

    first = early & (y == 0) & (z < 2)
    causal = iota((BLK, BLK), 1) <= iota((BLK, BLK), 0)
    own0 = pl.multiple_of(block_of(0) * BLK, BLK)

    def near_step(g, carry):
        for u in range(UNROLL):
            col = pl.multiple_of((g * UNROLL + u) * HEAD_DIM, HEAD_DIM)
            col2 = pl.multiple_of((g * UNROLL + u) * 2 * HEAD_DIM, 2 * HEAD_DIM)
            q = qb[0, :, pl.ds(col, HEAD_DIM)]
            s1 = nt(q, near[0, pl.ds(own0, BLK), 0:HEAD_DIM])
            s2 = nt(q, near[0, pl.ds(own0 + BLK, BLK), 0:HEAD_DIM])
            s2 = jnp.where(causal, s2, -jnp.inf)
            top = jnp.max(jnp.maximum(s1, s2), axis=1, keepdims=True) * SCALE
            p1, p2 = [jnp.exp2(x * SCALE - top).astype(BF) for x in (s1, s2)]
            o = mm(p1, near[0, pl.ds(own0, BLK), HEAD_DIM:]) + mm(p2, near[0, pl.ds(own0 + BLK, BLK), HEAD_DIM:])
            half_o[:, pl.ds(col2, 2 * HEAD_DIM)] = o
            half_m[:, pl.ds(col, HEAD_DIM)] = jnp.broadcast_to(top, (BLK, HEAD_DIM))
        return carry

    wide = UNROLL * HEAD_DIM
    halves = qb.shape[2] // wide

    def columns_of(head, g):
        return pl.ds(pl.multiple_of(head * qb.shape[2] + g * wide, wide), wide)

    def sent(i, g):
        return pltpu.make_async_remote_copy(
            src_ref=ob.at[i, :, pl.ds(pl.multiple_of(g * wide, wide), wide)],
            dst_ref=out.at[:, columns_of(heads_of(i), g)],
            send_sem=out_s.at[i, g],
            recv_sem=out_r.at[heads_of(i), g],
            device_id=(s, block_of(i)),
            device_id_type=MESH,
        )

    def arriving(source, g):
        block = out.at[:, columns_of(source, g)]
        return pltpu.make_async_remote_copy(
            src_ref=block,
            dst_ref=block,
            send_sem=out_s.at[0, g],
            recv_sem=out_r.at[source, g],
            device_id=(s, source),
            device_id_type=MESH,
        )

    def kept(i, g):
        return pltpu.make_async_copy(
            ob.at[i, :, pl.ds(pl.multiple_of(g * wide, wide), wide)],
            out.at[:, columns_of(heads_of(i), g)],
            out_s.at[i, g],
        )

    def mid_bias_of(block):
        return jnp.where((block - 1 - MIDB) * PER + iota((1, MIDS), 1) >= 0, 0.0, -jnp.inf)

    def coarse_bias_of(block):
        p = iota((1, coarse.shape[1]), 1)
        c = (p // (X * HERE)) % Y * (Z * X * HERE) + p // ROWS * (X * HERE) + p % (X * HERE)
        return jnp.where(c <= block - MIDB - 2, 0.0, -jnp.inf)

    def deliver(i, g):
        @pl.when(block_of(i) != h)
        def _():
            sent(i, g).start()

        @pl.when(block_of(i) == h)
        def _():
            kept(i, g).start()

    def first_step(g, carry):
        block = s * HERE + block_of(0)
        m0 = pl.multiple_of(block_of(0) * PER, PER)
        mid_bias, coarse_bias = mid_bias_of(block), coarse_bias_of(block)
        for u in range(UNROLL):
            col = pl.multiple_of((g * UNROLL + u) * HEAD_DIM, HEAD_DIM)
            col2 = pl.multiple_of((g * UNROLL + u) * 2 * HEAD_DIM, 2 * HEAD_DIM)
            q = qb[0, :, pl.ds(col, HEAD_DIM)]
            s3 = nt(q, mid[0, pl.ds(m0, MIDS), 0:HEAD_DIM]) + mid_bias
            s4 = nt(q, coarse[0, :, 0:HEAD_DIM]) + coarse_bias
            before = half_m[:, pl.ds(col, HEAD_DIM)][:, 0:1]
            top = jnp.maximum(jnp.max(jnp.maximum(s3, s4), axis=1, keepdims=True) * SCALE, before)
            p3, p4 = [jnp.exp2(x * SCALE - top).astype(BF) for x in (s3, s4)]
            o = half_o[:, pl.ds(col2, 2 * HEAD_DIM)] * jnp.exp2(before - top)
            o = o + mm(p3, mid[0, pl.ds(m0, MIDS), HEAD_DIM:]) + mm(p4, coarse[0, :, HEAD_DIM:])
            ob[0, :, pl.ds(col, HEAD_DIM)] = (o[:, :HEAD_DIM] / o[:, HEAD_DIM:]).astype(BF)
        deliver(0, g)
        pl.when((g == 0) & first & (s > 0))(send_far)
        return carry

    def near_part():
        q_load(0).wait()
        lax.fori_loop(0, halves, near_step, 0)

    @pl.when(s == 0)
    def _():
        near_part()
        lax.fori_loop(0, halves, first_step, 0)

    others = unit.at[pl.ds(0, PLANE - 1)]
    all_ones = pltpu.make_async_remote_copy(
        src_ref=others,
        dst_ref=others,
        send_sem=one_s,
        recv_sem=one_r,
        device_id=(in_plane(1), h),
        device_id_type=MESH,
    )
    all_ones.wait_recv()
    units = unit[...].reshape(PLANE * 16, HEAD_DIM)
    r, c = iota((ROWS, PLANE * 16), 0), iota((ROWS, PLANE * 16), 1)
    at = (r // HERE) * 16 + r % HERE
    pick_k = jnp.where(c == at, 1.0, 0.0).astype(BF)
    pick_v = jnp.where(c == at + HERE, 1.0, 0.0).astype(BF)
    coarse[0, plane_rows(z), 0:HEAD_DIM] = mm(pick_k, units).astype(BF)
    coarse[0, plane_rows(z), HEAD_DIM : 2 * HEAD_DIM] = mm(pick_v, units).astype(BF)

    low = jnp.where(y == 1, 0, z)
    lax.fori_loop(low, z, start_two, 0)
    above = half + Z // 2 - 1 - z
    pl.when(above > 0)(lambda: pl.semaphore_wait(ready_near, above))
    lax.fori_loop(z + 1, half + Z // 2, start_two, 0)

    pl.when(early & jnp.logical_not(first))(send_far)

    pl.when(s > 0)(near_part)
    for n in range(3):
        copy, step = halo(n)
        pl.when(s >= step)(copy.wait_recv)

    def got_two(k, carry):
        two(z, k).wait_recv()
        return carry

    lax.fori_loop(0, z, got_two, 0)
    lax.fori_loop(z + 1, jnp.where(y == 1, Z, z + 1), got_two, 0)
    for i in range(1, HERE):
        pl.when(i < taken)(q_load(i).wait)
    for n in (4, 5):
        pl.when(gives)(give(n).start)
    pl.when(gives & (s >= 1))(tail.wait_recv)
    pl.when(gives)(give(3).start)

    @pl.when(s > 0)
    def _():
        lax.fori_loop(0, halves, first_step, 0)

    pl.when(s == 0)(send_far)

    def step(t, carry):
        i, g = t // halves, t % halves
        j, k = block_of(i), context_of(i)
        block = s * HERE + j
        pl.when((j == 0) & (g == 0) & (s >= 1) & jnp.logical_not(gives))(tail.wait_recv)

        @pl.when(t == taken * halves)
        def _():
            for n in (0, 2, 3, 4, 5):
                give(n).wait_recv()

        pl.when(both & (t == 2 * halves))(give(6).wait_recv)
        pl.when(both & (t == 3 * halves))(give(1).wait_recv)
        r0 = pl.multiple_of(j * BLK, BLK)
        m0 = pl.multiple_of(j * PER, PER)
        before = jnp.where(block >= 1, 0.0, -jnp.inf)
        mid_bias, coarse_bias = mid_bias_of(block), coarse_bias_of(block)
        for u in range(UNROLL):
            col = pl.multiple_of((g * UNROLL + u) * HEAD_DIM, HEAD_DIM)
            q = qb[i, :, pl.ds(col, HEAD_DIM)]
            s1 = nt(q, near[k, pl.ds(r0, BLK), 0:HEAD_DIM]) + before
            s2 = nt(q, near[k, pl.ds(r0 + BLK, BLK), 0:HEAD_DIM])
            s2 = jnp.where(causal, s2, -jnp.inf)
            s3 = nt(q, mid[k, pl.ds(m0, MIDS), 0:HEAD_DIM]) + mid_bias
            s4 = nt(q, coarse[k, :, 0:HEAD_DIM]) + coarse_bias
            top = jnp.maximum(jnp.maximum(s1, s2), jnp.maximum(s3, s4))
            top = jnp.max(top, axis=1, keepdims=True) * SCALE
            p1, p2, p3, p4 = [jnp.exp2(x * SCALE - top).astype(BF) for x in (s1, s2, s3, s4)]
            o = mm(p1, near[k, pl.ds(r0, BLK), HEAD_DIM:]) + mm(p2, near[k, pl.ds(r0 + BLK, BLK), HEAD_DIM:])
            o = o + mm(p3, mid[k, pl.ds(m0, MIDS), HEAD_DIM:]) + mm(p4, coarse[k, :, HEAD_DIM:])
            ob[i, :, pl.ds(col, HEAD_DIM)] = (o[:, :HEAD_DIM] / o[:, HEAD_DIM:]).astype(BF)

        deliver(i, g)
        return carry

    lax.fori_loop(halves, HERE * halves, step, 0)

    for n in range(4):
        copy, step_up = halo(n)
        pl.when(s + step_up < devices)(copy.wait_send)

    def sent_two(k, carry):
        two(k, z).wait_send()
        return carry

    lax.fori_loop(low, z, sent_two, 0)
    lax.fori_loop(z + 1, Z, sent_two, 0)
    all_ones.wait_send()
    for n in (0, 2, 3, 4, 5):
        pl.when(gives)(give(n).wait_send)
    for n in (1, 6):
        pl.when(both)(give(n).wait_send)
    for g in range(halves):
        for i in range(HERE):
            pl.when(block_of(i) != h)(sent(i, g).wait_send)
            pl.when(block_of(i) == h)(kept(i, g).wait)
        for d in (1, 2, 3):
            other = (h + d) % 4
            pl.when(jnp.logical_not(both) | (d != 2))(arriving(other, g).wait_recv)


def settle(src, dst, buf, sem):
    n, rows = 8, src.shape[0] // 8
    parts = [pl.ds(i * rows, rows) for i in range(n)]
    ins = [pltpu.make_async_copy(src.at[p], buf.at[p], sem.at[0, i]) for i, p in enumerate(parts)]
    outs = [pltpu.make_async_copy(buf.at[p], dst.at[p], sem.at[1, i]) for i, p in enumerate(parts)]
    for c in ins:
        c.start()
    for a, b in zip(ins, outs):
        a.wait()
        b.start()
    for b in outs:
        b.wait()


def body(queries, keys, values, mid_pool, coarse_pool):
    rows, columns = queries.shape
    devices = lax.axis_size("seq")
    halves = columns // (UNROLL * HEAD_DIM)
    dma = pltpu.SemaphoreType.DMA
    hbm, any_ = pl.BlockSpec(memory_space=pltpu.HBM), pl.BlockSpec(memory_space=pl.ANY)
    landed = pl.pallas_call(
        kernel,
        out_shape=jax.ShapeDtypeStruct((rows // HERE, HERE * columns), BF),
        in_specs=[hbm] * 5,
        out_specs=any_,
        scratch_shapes=[
            pltpu.VMEM((HERE, BLK, columns), BF),
            pltpu.VMEM((HERE, BLK, columns), BF),
            pltpu.VMEM((BLK, 2 * columns), F32),
            pltpu.VMEM((BLK, columns), F32),
            pltpu.VMEM((2, (HERE + 1) * BLK, 384), BF),
            pltpu.VMEM((HERE * PER, 256), BF),
            pltpu.VMEM((2, 352, 384), BF),
            pltpu.VMEM((2, devices * HERE, 384), BF),
            pltpu.VMEM((PLANE, 16, HEAD_DIM), BF),
            pltpu.VMEM((1, GROUP), BF),
            pltpu.VMEM((1, BLK), BF),
            dma((4,)),
            dma((HERE,)),
            dma((4,)),
            dma((4,)),
            dma,
            dma,
            dma((Z,)),
            dma((Z,)),
            pltpu.SemaphoreType.REGULAR,
            pltpu.SemaphoreType.REGULAR,
            dma((7,)),
            dma((7,)),
            dma((HERE, halves)),
            dma((4, halves)),
        ],
        compiler_params=pltpu.CompilerParams(
            collective_id=0, has_side_effects=True, vmem_limit_bytes=60 * 2**20
        ),
    )(queries, keys, values, mid_pool, coarse_pool)
    return pl.pallas_call(
        settle,
        out_shape=jax.ShapeDtypeStruct(landed.shape, BF),
        in_specs=[any_],
        out_specs=any_,
        scratch_shapes=[pltpu.VMEM(landed.shape, BF), dma((2, 8))],
        compiler_params=pltpu.CompilerParams(vmem_limit_bytes=60 * 2**20),
    )(landed)


def solution(mesh):
    return jax.shard_map(
        body,
        mesh=mesh,
        in_specs=(
            P("seq", "head"),
            P("seq", "head"),
            P("seq", "head"),
            P("head", None),
            P("head", None),
        ),
        out_specs=P(("seq", "head"), None),
        check_vma=False,
    )
```

```python
import math

import jax
import jax.numpy as jnp
from jax import lax
from jax.experimental import pallas as pl
from jax.experimental.pallas import tpu as pltpu
from jax.sharding import PartitionSpec as P

HEAD_DIM = 128
BLK = 256
GROUP = 8
PER = BLK // GROUP
MIDB = 8
MIDS = 256
HERE = 4
X, Z, Y = 4, 8, 2
PLANE = X * Y
ROWS = PLANE * HERE
UNROLL = 4
MESH = pl.DeviceIdType.MESH
BF = jnp.bfloat16
F32 = jnp.float32
SCALE = math.log2(math.e) / math.sqrt(HEAD_DIM)


def nt(a, b):
    return lax.dot_general(a, b, (((1,), (1,)), ((), ())), preferred_element_type=F32)


def mm(a, b):
    return jnp.dot(a, b, preferred_element_type=F32)


def iota(shape, dim):
    return lax.broadcasted_iota(jnp.int32, shape, dim)


def pool_matrix(mid_ref, coarse_ref):
    row, col = iota((48, BLK), 0), iota((48, BLK), 1)
    mids = mid_ref[...].astype(F32)
    spread = jnp.zeros((1, BLK), F32)
    lane = iota((1, BLK), 1) % GROUP
    for t in range(GROUP):
        spread = jnp.where(lane == t, mids[0:1, t : t + 1], spread)
    w = jnp.where((row < PER) & (col // GROUP == row), spread, 0.0)
    return jnp.where(row == PER, coarse_ref[...].astype(F32), w).astype(BF)


def kernel(
    queries,
    keys,
    values,
    mid_pool,
    coarse_pool,
    out,
    qb,
    ob,
    half_o,
    half_m,
    near,
    mymid,
    mid,
    coarse,
    unit,
    mid_w,
    coarse_w,
    in_sem,
    q_sem,
    halo_s,
    halo_r,
    one_s,
    one_r,
    two_s,
    two_r,
    ready_near,
    ready_far,
    ctx_s,
    ctx_r,
    out_s,
    out_r,
):
    s, h = lax.axis_index("seq"), lax.axis_index("head")
    devices = lax.axis_size("seq")
    y, z, x = s // (Z * X), (s // X) % Z, s % X
    u = y * X + x
    yh, core = h // 2, h % 2
    early = z < Z // 2

    def in_plane(i):
        v = (u + i) % PLANE
        return (v // X) * (Z * X) + z * X + v % X

    def at_z(k):
        return (y * Z + k) * X + x

    gives = (core == 1) & (s > 0)
    both = gives & (y == 1)
    taken = jnp.where(gives, 3 - y, HERE)
    partner = h + 2 - 4 * yh

    def block_of(i):
        odd, even = (1 - yh) * 2 + 1, (1 - yh) * 2
        other, own = yh * 2 + 1 - core, yh * 2 + core

        late = (y == 1) & (z >= 2)

        def pick(*blocks):
            return jnp.where(i == 0, blocks[0], jnp.where(i == 1, blocks[1], jnp.where(i == 2, blocks[2], blocks[3])))

        giving = jnp.where(y == 1, pick(own, other, other, own), pick(odd, other, own, other))
        return jnp.where(gives, giving, jnp.where(late, pick(other, odd, even, own), jnp.where(y == 1, pick(odd, other, even, own), pick(odd, even, other, own))))

    def context_of(i):
        return jnp.where(i >= taken, 1, 0)

    def heads_of(i):
        return jnp.where(i >= taken, partner, h)

    loads = [
        pltpu.make_async_copy(keys, near.at[0, pl.ds(BLK, HERE * BLK), pl.ds(0, HEAD_DIM)], in_sem.at[0]),
        pltpu.make_async_copy(
            values, near.at[0, pl.ds(BLK, HERE * BLK), pl.ds(HEAD_DIM, HEAD_DIM)], in_sem.at[1]
        ),
        pltpu.make_async_copy(mid_pool, mid_w, in_sem.at[2]),
        pltpu.make_async_copy(coarse_pool, coarse_w, in_sem.at[3]),
    ]
    for c in loads:
        c.start()

    def q_load(i):
        return pltpu.make_async_copy(
            queries.at[pl.ds(pl.multiple_of(block_of(i) * BLK, BLK), BLK)], qb.at[i], q_sem.at[i]
        )

    barrier = pltpu.get_barrier_semaphore()

    def tell(seq, head):
        pl.semaphore_signal(barrier, inc=1, device_id=(seq, head), device_id_type=MESH)

    for i in range(1, 4):
        tell(s, (h + i) % 4)
    for i in range(1, PLANE):
        tell(in_plane(i), h)
    for back in (1, 2, 3):

        @pl.when(s >= back)
        def _():
            tell(s - back, h)

    def tell_upper(k, carry):
        tell(at_z(k), h)
        return carry

    lax.fori_loop(z + 1, Z, tell_upper, 0)

    def blank(ref, start, size):
        ref[0, pl.ds(start, size), 0 : 2 * HEAD_DIM] = jnp.zeros((size, 2 * HEAD_DIM), BF)

    pl.when(s < 1)(lambda: blank(near, 0, BLK))
    pl.when(s < 1)(lambda: blank(coarse, 0, ROWS))

    @pl.when(y == 0)
    def _():
        for k in range(Z):
            half = pl.ds(k * ROWS + X * HERE, ROWS - X * HERE)
            coarse[1, half, 0 : 2 * HEAD_DIM] = jnp.zeros((ROWS - X * HERE, 2 * HEAD_DIM), BF)
    pl.when(s < 1)(lambda: blank(mid, 160, 128))
    pl.when(s < 2)(lambda: blank(mid, 32, 128))
    pl.when(s < 3)(lambda: blank(mid, 0, 32))

    def blank_coarse(k, carry):
        blank(coarse, pl.multiple_of(k * ROWS, ROWS), ROWS)
        return carry

    lax.fori_loop(jnp.where(y == 0, z + 1, Z), Z, blank_coarse, 0)

    for ref in (near, mid, coarse):
        for k in range(2):
            ref[k, :, 2 * HEAD_DIM :] = jnp.ones((ref.shape[1], HEAD_DIM), BF)
    for c in loads:
        c.wait()
    for i in range(HERE):
        pl.when(i < taken)(q_load(i).start)
    pooling = pool_matrix(mid_w, coarse_w)
    tops = []
    for j in range(HERE):
        pooled = mm(pooling, near[0, BLK + j * BLK : 2 * BLK + j * BLK, 0 : 2 * HEAD_DIM])
        mymid[j * PER : (j + 1) * PER, :] = pooled[0:PER].astype(BF)
        if j < 2:
            mid[0, 288 + j * PER : 288 + (j + 1) * PER, 0 : 2 * HEAD_DIM] = pooled[0:PER].astype(BF)
        tops.append(pooled[PER : PER + 1])
    rows = [t[:, :HEAD_DIM] for t in tops] + [t[:, HEAD_DIM:] for t in tops]
    mine = jnp.zeros((16, HEAD_DIM), F32)
    for n, r in enumerate(rows):
        mine = jnp.where(iota((16, HEAD_DIM), 0) == n, r, mine)
    unit[u] = mine.astype(BF)

    pl.semaphore_wait(barrier, 3 + (PLANE - 1) + z + jnp.minimum(3, devices - 1 - s))

    half = z - z % (Z // 2)

    def tell_ready(sem):
        def tell_one(k, carry):
            pl.semaphore_signal(sem, inc=1, device_id=(at_z(k), h), device_id_type=MESH)
            return carry

        return tell_one

    lax.fori_loop(half, z, tell_ready(ready_near), 0)
    lax.fori_loop(0, half, tell_ready(ready_far), 0)

    def one(i):
        return pltpu.make_async_remote_copy(
            src_ref=unit.at[u],
            dst_ref=unit.at[u],
            send_sem=one_s,
            recv_sem=one_r,
            device_id=(in_plane(i), h),
            device_id_type=MESH,
        )

    def halo(n):
        src, dst, step = (
            (mymid, mid.at[0, pl.ds(160, 128), pl.ds(0, 256)], 1),
            (mymid, mid.at[0, pl.ds(32, 128), pl.ds(0, 256)], 2),
            (mymid.at[pl.ds(96, 32)], mid.at[0, pl.ds(0, 32), pl.ds(0, 256)], 3),
            (
                near.at[0, pl.ds(HERE * BLK, BLK), pl.ds(0, 256)],
                near.at[0, pl.ds(0, BLK), pl.ds(0, 256)],
                1,
            ),
        )[n]
        copy = pltpu.make_async_remote_copy(
            src_ref=src,
            dst_ref=dst,
            send_sem=halo_s.at[n],
            recv_sem=halo_r.at[n],
            device_id=(s + step, h),
            device_id_type=MESH,
        )
        return copy, step

    def give(n):
        away = 1 - yh
        even = pl.multiple_of(away * 2 * BLK, 2 * BLK)
        src, dst = (
            (queries.at[pl.ds(even, BLK)], qb.at[jnp.where(both, 2, 3)]),
            (queries.at[pl.ds(even + BLK, BLK)], qb.at[3]),
            tuple(near.at[k, pl.ds(even + BLK, BLK), pl.ds(0, 256)] for k in (0, 1)),
            tuple(near.at[k, pl.ds(even, BLK), pl.ds(0, 256)] for k in (0, 1)),
            tuple(mid.at[k, pl.ds(pl.multiple_of(away * 64, 64), 288), pl.ds(0, 256)] for k in (0, 1)),
            tuple(coarse.at[k, :, pl.ds(0, 256)] for k in (0, 1)),
            tuple(near.at[k, pl.ds(even + 2 * BLK, BLK), pl.ds(0, 256)] for k in (0, 1)),
            tuple(coarse.reshape(2, Z, ROWS, 384).at[k, :, pl.ds(0, X * HERE), pl.ds(0, 256)] for k in (0, 1)),
        )[n]
        return pltpu.make_async_remote_copy(
            src_ref=src,
            dst_ref=dst,
            send_sem=ctx_s.at[n],
            recv_sem=ctx_r.at[n],
            device_id=(s, partner),
            device_id_type=MESH,
        )

    def plane_rows(k):
        return pl.ds(pl.multiple_of(k * ROWS, ROWS), ROWS)

    def two(k, of):
        block = coarse.at[0, plane_rows(of), pl.ds(0, 256)]
        return pltpu.make_async_remote_copy(
            src_ref=block,
            dst_ref=block,
            send_sem=two_s.at[k],
            recv_sem=two_r.at[of],
            device_id=(at_z(k), h),
            device_id_type=MESH,
        )

    for i in range(1, PLANE):
        one(i).start()
    for n in range(3):
        copy, step = halo(n)
        pl.when(s + step < devices)(copy.start)
    tail, _ = halo(3)
    pl.when(s + 1 < devices)(tail.start)
    for n in (2, 0):
        pl.when(gives)(give(n).start)
    for n in (6, 1):
        pl.when(both)(give(n).start)
    def start_two(k, carry):
        two(k, z).start()
        return carry

    def send_far():
        pl.semaphore_wait(ready_far, Z // 2)
        lax.fori_loop(Z // 2, Z, start_two, 0)

    first = early & (y == 0) & (z < 2)
    causal = iota((BLK, BLK), 1) <= iota((BLK, BLK), 0)
    own0 = pl.multiple_of(block_of(0) * BLK, BLK)

    def near_step(g, carry):
        for u in range(UNROLL):
            col = pl.multiple_of((g * UNROLL + u) * HEAD_DIM, HEAD_DIM)
            col2 = pl.multiple_of((g * UNROLL + u) * 2 * HEAD_DIM, 2 * HEAD_DIM)
            q = qb[0, :, pl.ds(col, HEAD_DIM)]
            s1 = nt(q, near[0, pl.ds(own0, BLK), 0:HEAD_DIM])
            s2 = nt(q, near[0, pl.ds(own0 + BLK, BLK), 0:HEAD_DIM])
            s2 = jnp.where(causal, s2, -jnp.inf)
            top = jnp.max(jnp.maximum(s1, s2), axis=1, keepdims=True) * SCALE
            p1, p2 = [jnp.exp2(x * SCALE - top).astype(BF) for x in (s1, s2)]
            o = mm(p1, near[0, pl.ds(own0, BLK), HEAD_DIM:]) + mm(p2, near[0, pl.ds(own0 + BLK, BLK), HEAD_DIM:])
            half_o[:, pl.ds(col2, 2 * HEAD_DIM)] = o
            half_m[:, pl.ds(col, HEAD_DIM)] = jnp.broadcast_to(top, (BLK, HEAD_DIM))
        return carry

    wide = UNROLL * HEAD_DIM
    halves = qb.shape[2] // wide

    def columns_of(head, g):
        return pl.ds(pl.multiple_of(head * qb.shape[2] + g * wide, wide), wide)

    def sent(i, g):
        return pltpu.make_async_remote_copy(
            src_ref=ob.at[i, :, pl.ds(pl.multiple_of(g * wide, wide), wide)],
            dst_ref=out.at[:, columns_of(heads_of(i), g)],
            send_sem=out_s.at[i, g],
            recv_sem=out_r.at[heads_of(i), g],
            device_id=(s, block_of(i)),
            device_id_type=MESH,
        )

    def arriving(source, g):
        block = out.at[:, columns_of(source, g)]
        return pltpu.make_async_remote_copy(
            src_ref=block,
            dst_ref=block,
            send_sem=out_s.at[0, g],
            recv_sem=out_r.at[source, g],
            device_id=(s, source),
            device_id_type=MESH,
        )

    def kept(i, g):
        return pltpu.make_async_copy(
            ob.at[i, :, pl.ds(pl.multiple_of(g * wide, wide), wide)],
            out.at[:, columns_of(heads_of(i), g)],
            out_s.at[i, g],
        )

    def mid_bias_of(block):
        return jnp.where((block - 1 - MIDB) * PER + iota((1, MIDS), 1) >= 0, 0.0, -jnp.inf)

    def coarse_bias_of(block):
        p = iota((1, coarse.shape[1]), 1)
        c = (p // (X * HERE)) % Y * (Z * X * HERE) + p // ROWS * (X * HERE) + p % (X * HERE)
        return jnp.where(c <= block - MIDB - 2, 0.0, -jnp.inf)

    def deliver(i, g):
        @pl.when(block_of(i) != h)
        def _():
            sent(i, g).start()

        @pl.when(block_of(i) == h)
        def _():
            kept(i, g).start()

    def first_step(g, carry):
        block = s * HERE + block_of(0)
        m0 = pl.multiple_of(block_of(0) * PER, PER)
        mid_bias, coarse_bias = mid_bias_of(block), coarse_bias_of(block)
        for u in range(UNROLL):
            col = pl.multiple_of((g * UNROLL + u) * HEAD_DIM, HEAD_DIM)
            col2 = pl.multiple_of((g * UNROLL + u) * 2 * HEAD_DIM, 2 * HEAD_DIM)
            q = qb[0, :, pl.ds(col, HEAD_DIM)]
            s3 = nt(q, mid[0, pl.ds(m0, MIDS), 0:HEAD_DIM]) + mid_bias
            s4 = nt(q, coarse[0, :, 0:HEAD_DIM]) + coarse_bias
            before = half_m[:, pl.ds(col, HEAD_DIM)][:, 0:1]
            top = jnp.maximum(jnp.max(jnp.maximum(s3, s4), axis=1, keepdims=True) * SCALE, before)
            p3, p4 = [jnp.exp2(x * SCALE - top).astype(BF) for x in (s3, s4)]
            o = half_o[:, pl.ds(col2, 2 * HEAD_DIM)] * jnp.exp2(before - top)
            o = o + mm(p3, mid[0, pl.ds(m0, MIDS), HEAD_DIM:]) + mm(p4, coarse[0, :, HEAD_DIM:])
            ob[0, :, pl.ds(col, HEAD_DIM)] = (o[:, :HEAD_DIM] / o[:, HEAD_DIM:]).astype(BF)
        deliver(0, g)
        pl.when((g == 0) & first & (s > 0))(send_far)
        return carry

    def near_part():
        q_load(0).wait()
        lax.fori_loop(0, halves, near_step, 0)

    @pl.when(s == 0)
    def _():
        near_part()
        lax.fori_loop(0, halves, first_step, 0)

    others = unit.at[pl.ds(0, PLANE - 1)]
    all_ones = pltpu.make_async_remote_copy(
        src_ref=others,
        dst_ref=others,
        send_sem=one_s,
        recv_sem=one_r,
        device_id=(in_plane(1), h),
        device_id_type=MESH,
    )
    all_ones.wait_recv()
    units = unit[...].reshape(PLANE * 16, HEAD_DIM)
    r, c = iota((ROWS, PLANE * 16), 0), iota((ROWS, PLANE * 16), 1)
    at = (r // HERE) * 16 + r % HERE
    pick_k = jnp.where(c == at, 1.0, 0.0).astype(BF)
    pick_v = jnp.where(c == at + HERE, 1.0, 0.0).astype(BF)
    coarse[0, plane_rows(z), 0:HEAD_DIM] = mm(pick_k, units).astype(BF)
    coarse[0, plane_rows(z), HEAD_DIM : 2 * HEAD_DIM] = mm(pick_v, units).astype(BF)

    low = jnp.where(y == 1, 0, z)
    lax.fori_loop(low, z, start_two, 0)
    above = half + Z // 2 - 1 - z
    pl.when(above > 0)(lambda: pl.semaphore_wait(ready_near, above))
    lax.fori_loop(z + 1, half + Z // 2, start_two, 0)

    pl.when(early & jnp.logical_not(first))(send_far)

    pl.when(s > 0)(near_part)
    for n in range(3):
        copy, step = halo(n)
        pl.when(s >= step)(copy.wait_recv)

    def got_two(k, carry):
        two(z, k).wait_recv()
        return carry

    lax.fori_loop(0, z, got_two, 0)
    lax.fori_loop(z + 1, jnp.where(y == 1, Z, z + 1), got_two, 0)
    for i in range(1, HERE):
        pl.when(i < taken)(q_load(i).wait)
    pl.when(gives)(give(4).start)
    pl.when(both)(give(5).start)
    pl.when(gives & (y == 0))(give(7).start)
    pl.when(gives & (s >= 1))(tail.wait_recv)
    pl.when(gives)(give(3).start)

    @pl.when(s > 0)
    def _():
        lax.fori_loop(0, halves, first_step, 0)

    pl.when(s == 0)(send_far)

    def step(t, carry):
        i, g = t // halves, t % halves
        j, k = block_of(i), context_of(i)
        block = s * HERE + j
        pl.when((j == 0) & (g == 0) & (s >= 1) & jnp.logical_not(gives))(tail.wait_recv)

        @pl.when(t == taken * halves)
        def _():
            for n in (0, 2, 3, 4):
                give(n).wait_recv()
            pl.when(y == 1)(give(5).wait_recv)
            pl.when(y == 0)(give(7).wait_recv)

        pl.when(both & (t == 2 * halves))(give(6).wait_recv)
        pl.when(both & (t == 3 * halves))(give(1).wait_recv)
        r0 = pl.multiple_of(j * BLK, BLK)
        m0 = pl.multiple_of(j * PER, PER)
        before = jnp.where(block >= 1, 0.0, -jnp.inf)
        mid_bias, coarse_bias = mid_bias_of(block), coarse_bias_of(block)
        for u in range(UNROLL):
            col = pl.multiple_of((g * UNROLL + u) * HEAD_DIM, HEAD_DIM)
            q = qb[i, :, pl.ds(col, HEAD_DIM)]
            s1 = nt(q, near[k, pl.ds(r0, BLK), 0:HEAD_DIM]) + before
            s2 = nt(q, near[k, pl.ds(r0 + BLK, BLK), 0:HEAD_DIM])
            s2 = jnp.where(causal, s2, -jnp.inf)
            s3 = nt(q, mid[k, pl.ds(m0, MIDS), 0:HEAD_DIM]) + mid_bias
            s4 = nt(q, coarse[k, :, 0:HEAD_DIM]) + coarse_bias
            top = jnp.maximum(jnp.maximum(s1, s2), jnp.maximum(s3, s4))
            top = jnp.max(top, axis=1, keepdims=True) * SCALE
            p1, p2, p3, p4 = [jnp.exp2(x * SCALE - top).astype(BF) for x in (s1, s2, s3, s4)]
            o = mm(p1, near[k, pl.ds(r0, BLK), HEAD_DIM:]) + mm(p2, near[k, pl.ds(r0 + BLK, BLK), HEAD_DIM:])
            o = o + mm(p3, mid[k, pl.ds(m0, MIDS), HEAD_DIM:]) + mm(p4, coarse[k, :, HEAD_DIM:])
            ob[i, :, pl.ds(col, HEAD_DIM)] = (o[:, :HEAD_DIM] / o[:, HEAD_DIM:]).astype(BF)

        deliver(i, g)
        return carry

    lax.fori_loop(halves, HERE * halves, step, 0)

    for n in range(4):
        copy, step_up = halo(n)
        pl.when(s + step_up < devices)(copy.wait_send)

    def sent_two(k, carry):
        two(k, z).wait_send()
        return carry

    lax.fori_loop(low, z, sent_two, 0)
    lax.fori_loop(z + 1, Z, sent_two, 0)
    all_ones.wait_send()
    for n in (0, 2, 3, 4):
        pl.when(gives)(give(n).wait_send)
    for n in (1, 5, 6):
        pl.when(both)(give(n).wait_send)
    pl.when(gives & (y == 0))(give(7).wait_send)
    for g in range(halves):
        for i in range(HERE):
            pl.when(block_of(i) != h)(sent(i, g).wait_send)
            pl.when(block_of(i) == h)(kept(i, g).wait)
        for d in (1, 2, 3):
            other = (h + d) % 4
            pl.when(jnp.logical_not(both) | (d != 2))(arriving(other, g).wait_recv)


def settle(src, dst, buf, sem):
    n, rows = 8, src.shape[0] // 8
    parts = [pl.ds(i * rows, rows) for i in range(n)]
    ins = [pltpu.make_async_copy(src.at[p], buf.at[p], sem.at[0, i]) for i, p in enumerate(parts)]
    outs = [pltpu.make_async_copy(buf.at[p], dst.at[p], sem.at[1, i]) for i, p in enumerate(parts)]
    for c in ins:
        c.start()
    for a, b in zip(ins, outs):
        a.wait()
        b.start()
    for b in outs:
        b.wait()


def body(queries, keys, values, mid_pool, coarse_pool):
    rows, columns = queries.shape
    devices = lax.axis_size("seq")
    halves = columns // (UNROLL * HEAD_DIM)
    dma = pltpu.SemaphoreType.DMA
    hbm, any_ = pl.BlockSpec(memory_space=pltpu.HBM), pl.BlockSpec(memory_space=pl.ANY)
    landed = pl.pallas_call(
        kernel,
        out_shape=jax.ShapeDtypeStruct((rows // HERE, HERE * columns), BF),
        in_specs=[hbm] * 5,
        out_specs=any_,
        scratch_shapes=[
            pltpu.VMEM((HERE, BLK, columns), BF),
            pltpu.VMEM((HERE, BLK, columns), BF),
            pltpu.VMEM((BLK, 2 * columns), F32),
            pltpu.VMEM((BLK, columns), F32),
            pltpu.VMEM((2, (HERE + 1) * BLK, 384), BF),
            pltpu.VMEM((HERE * PER, 256), BF),
            pltpu.VMEM((2, 352, 384), BF),
            pltpu.VMEM((2, devices * HERE, 384), BF),
            pltpu.VMEM((PLANE, 16, HEAD_DIM), BF),
            pltpu.VMEM((1, GROUP), BF),
            pltpu.VMEM((1, BLK), BF),
            dma((4,)),
            dma((HERE,)),
            dma((4,)),
            dma((4,)),
            dma,
            dma,
            dma((Z,)),
            dma((Z,)),
            pltpu.SemaphoreType.REGULAR,
            pltpu.SemaphoreType.REGULAR,
            dma((8,)),
            dma((8,)),
            dma((HERE, halves)),
            dma((4, halves)),
        ],
        compiler_params=pltpu.CompilerParams(
            collective_id=0, has_side_effects=True, vmem_limit_bytes=60 * 2**20
        ),
    )(queries, keys, values, mid_pool, coarse_pool)
    return pl.pallas_call(
        settle,
        out_shape=jax.ShapeDtypeStruct(landed.shape, BF),
        in_specs=[any_],
        out_specs=any_,
        scratch_shapes=[pltpu.VMEM(landed.shape, BF), dma((2, 8))],
        compiler_params=pltpu.CompilerParams(vmem_limit_bytes=60 * 2**20),
    )(landed)


def solution(mesh):
    return jax.shard_map(
        body,
        mesh=mesh,
        in_specs=(
            P("seq", "head"),
            P("seq", "head"),
            P("seq", "head"),
            P("head", None),
            P("head", None),
        ),
        out_specs=P(("seq", "head"), None),
        check_vma=False,
    )
```
